128 devices in a mesh: seq: 16 (over y, z_hi, core), tensor: 8 (over z_lo, x).
Axes of the slice: x: 4, y: 4, z: 4 (z_hi: 2, z_lo: 2; z = z_hi * 2 + z_lo), core: 2. Of those that a mesh axis runs over, the one named last changes fastest.
Arguments:
- queries: bfloat16 [2048, 4096], P('seq', 'tensor'), may hold values from -32 to 32
- key_rows: bfloat16 [2048, 1024], P('seq', 'tensor'), may hold values from -32 to 32
- values: bfloat16 [2048, 1024], P('seq', 'tensor'), may hold values from -6 to 6
- out_weight: bfloat16 [4096, 8192], P('tensor'), may hold values from -0.09375 to 0.09375
- out_grad: bfloat16 [2048, 8192], P(('seq', 'tensor')), may hold values from -6 to 6
- doc_lengths: int32 [12], replicated, may hold values from 1 to 1024, 2048 in all
Outputs:
- projected: bfloat16 [2048, 8192], P(('seq', 'tensor'))
- query_grad: bfloat16 [2048, 4096], P('seq', 'tensor')
- key_grad: bfloat16 [2048, 1024], P('seq', 'tensor')
- value_grad: bfloat16 [2048, 1024], P('seq', 'tensor')
The draws below stay inside these ranges and needn't reach their ends.
Inputs may be any that keep to these rules, and one draw needn't show every extreme that they name: `doc_lengths`: 12 document lengths, each 1 or more, summing to 2048; the longest is exactly 1024.
All inputs are finite; a program needn't handle non-finite values.
Results may differ from the reference program's by a relative error of at most 0.03.
Values may be sent and summed in bfloat16 or wider, within the bound.
A program may use at most 64 MiB of HBM per device.

```python
import math
import jax
import jax.numpy as jnp
import numpy as np
from jax import lax

D = 8192
QHEADS = 32
KVHEADS = 8
HEAD = 128
DOCS = 12
TOKENS = 2048
LONGEST = 1024
N_TENSOR = 8


def draw_key_rows(key, part):
    own_key = jax.random.fold_in(key, 3)
    return jax.random.truncated_normal(own_key, -6.0, 6.0, (TOKENS, KVHEADS * HEAD), jnp.float32).astype(jnp.bfloat16)


def draw_queries(key, part):
    own_key = jax.random.fold_in(key, 5)
    return jax.random.truncated_normal(own_key, -6.0, 6.0, (TOKENS, QHEADS * HEAD), jnp.float32).astype(jnp.bfloat16)


def block_scale(key, shape, cuts, smallest, high):
    level, own = 1.0, jax.random.fold_in(key, 6)
    for dim, blocks in cuts:
        draws = jnp.exp(jax.random.uniform(jax.random.fold_in(own, dim), (blocks,), jnp.float32, smallest / len(cuts), high / len(cuts)))
        level = level * jnp.repeat(draws, shape[dim] // blocks).reshape([-1 if axis == dim else 1 for axis in range(len(shape))])
    return level


def profile(count, total, limit, slope):
    portions = [(1 << 20) // math.isqrt(standing ** slope) + 1 for standing in range(2, count + 1)]
    rest, given = total - limit - (count - 1), [1] * (count - 1)
    while rest > 0:
        candidates = [i for i in range(count - 1) if given[i] < limit]
        whole, remaining = sum([portions[i] for i in candidates]), rest
        for i in candidates:
            more = min(limit - given[i], max(1, remaining * portions[i] // whole), rest)
            given[i] = given[i] + more
            rest = rest - more
    return np.array([limit] + given)


def ragged(stream_key, amount, total, bound, lean):
    if amount == 2:
        one = jax.random.randint(stream_key, (), max(1, total - bound), min(bound, total - 1) + 1)
        return jnp.stack([one, total - one])
    lengths = jnp.asarray(profile(amount, total, bound, lean), jnp.int32)
    pairs = (amount - 1) // 2
    source_of, taker = lengths[1:1 + 2 * pairs:2], lengths[2:2 + 2 * pairs:2]
    slack = jnp.minimum(source_of - 1, bound - taker)
    moved = jax.random.randint(jax.random.fold_in(stream_key, 1), (pairs,), 0, 1 << 20) % (slack + 1)
    lengths = lengths.at[1:1 + 2 * pairs:2].set(source_of - moved).at[2:2 + 2 * pairs:2].set(taker + moved)
    return lengths[jax.random.permutation(jax.random.fold_in(stream_key, 2), amount)]


def bell_draw(rng, extent, spread, bound, pieces=(), kind=jnp.bfloat16):
    result = jax.random.normal(rng, extent, jnp.float32) * spread
    if len(pieces) > 0:
        result = block_scale(rng, extent, pieces, -0.22, 0.18) * result
    return jnp.clip(result, min=-bound, max=bound).astype(kind)


def setup_inputs(seed: int = 0) -> dict:
    streams_of = jax.random.split(jax.random.key(seed), 7)
    return {
        "queries": draw_queries(jax.random.fold_in(streams_of[6], 71), 0),
        "key_rows": draw_key_rows(jax.random.fold_in(streams_of[6], 71), 0),
        "values": bell_draw(streams_of[2], (TOKENS, KVHEADS * HEAD), 1.0, 6.0, ((0, 16), (1, 8))),
        "out_weight": bell_draw(streams_of[3], (QHEADS * HEAD, D), (QHEADS * HEAD) ** -0.5, 0.09375, ((0, 8),)),
        "out_grad": bell_draw(streams_of[4], (TOKENS, D), 1.0, 6.0, ((0, 128),)),
        "doc_lengths": ragged(streams_of[5], DOCS, TOKENS, LONGEST, 2).astype(jnp.int32),
    }


def doc_index(doc_lengths, token_total):
    doc_ends = jnp.cumsum(doc_lengths).astype(jnp.int32)
    positions = jnp.arange(token_total, dtype=jnp.int32)
    return lax.optimization_barrier(jnp.sum((doc_ends[:, None] <= positions[None, :]).astype(jnp.int32), axis=0)).astype(jnp.int32)

def reference(queries, key_rows, values, out_weight, out_grad, doc_lengths):
    group_size = QHEADS // KVHEADS
    score_scale = 1.0 / math.sqrt(HEAD)
    documents = doc_index(doc_lengths, TOKENS)
    positions = jnp.arange(TOKENS, dtype=jnp.int32)
    allowed = (documents[:, None] == documents[None, :]) & (positions[None, :] <= positions[:, None])
    query_heads = queries.reshape(TOKENS, QHEADS, HEAD).transpose(1, 0, 2)
    key_heads = jnp.repeat(key_rows.reshape(TOKENS, KVHEADS, HEAD).transpose(1, 0, 2), group_size, axis=0)
    value_heads = jnp.repeat(values.reshape(TOKENS, KVHEADS, HEAD).transpose(1, 0, 2), group_size, axis=0)
    contract_last = (((1,), (1,)), ((), ()))
    contract_first = (((0,), (0,)), ((), ()))

    def forward_head(operands):
        query_one, key_one, value_one = operands
        scores = lax.dot_general(query_one, key_one, contract_last, preferred_element_type=jnp.float32) * score_scale
        masked_scores = jnp.where(allowed, scores, jnp.float32(-1e+30))
        row_peak = lax.optimization_barrier(jnp.max(masked_scores, axis=1))
        row_total = lax.optimization_barrier(jnp.sum(jnp.where(allowed, jnp.exp(masked_scores - row_peak[:, None]), jnp.float32(0.0)), axis=1))
        log_total = row_peak + jnp.log(row_total)
        weights = jnp.where(allowed, jnp.exp(scores - log_total[:, None]), jnp.float32(0.0))
        mixed = jnp.dot(weights, value_one.astype(jnp.float32), precision=lax.Precision.HIGHEST, preferred_element_type=jnp.float32).astype(jnp.bfloat16)
        return (mixed, log_total)
    attn_heads, log_totals = lax.map(forward_head, (query_heads, key_heads, value_heads))
    attended = attn_heads.transpose(1, 0, 2).reshape(TOKENS, QHEADS * HEAD)
    head_cols = QHEADS * HEAD // N_TENSOR
    projected = jnp.zeros((TOKENS, D), jnp.float32)
    for member in range(N_TENSOR):
        partial_sum = jnp.dot(attended[:, member * head_cols:(member + 1) * head_cols], out_weight[member * head_cols:(member + 1) * head_cols, :], preferred_element_type=jnp.float32).astype(jnp.bfloat16)
        partial_sum = lax.optimization_barrier(partial_sum)
        projected = projected + partial_sum.astype(jnp.float32)
    projected = projected.astype(jnp.bfloat16)
    attn_grad = lax.dot_general(out_grad, out_weight, contract_last, preferred_element_type=jnp.float32).astype(jnp.bfloat16)
    grad_heads = attn_grad.reshape(TOKENS, QHEADS, HEAD).transpose(1, 0, 2)
    row_delta = lax.optimization_barrier(jnp.sum(grad_heads.astype(jnp.float32) * attn_heads.astype(jnp.float32), axis=-1))

    def backward_head(operands):
        query_one, key_one, value_one, grad_one, log_one, delta_one = operands
        scores = lax.dot_general(query_one, key_one, contract_last, preferred_element_type=jnp.float32) * score_scale
        probs = jnp.where(allowed, jnp.exp(scores - log_one[:, None]), jnp.float32(0.0))
        slopes = lax.dot_general(grad_one, value_one, contract_last, preferred_element_type=jnp.float32)
        score_grad = (probs * (slopes - delta_one[:, None]) * score_scale).astype(jnp.bfloat16)
        query_part = jnp.dot(score_grad, key_one, preferred_element_type=jnp.float32)
        key_part = lax.dot_general(score_grad, query_one, contract_first, preferred_element_type=jnp.float32)
        value_part = lax.dot_general(probs.astype(jnp.bfloat16), grad_one, contract_first, preferred_element_type=jnp.float32)
        return (query_part, key_part, value_part)
    query_parts, key_parts, value_parts = lax.map(backward_head, (query_heads, key_heads, value_heads, grad_heads, log_totals, row_delta))
    query_grad = query_parts.transpose(1, 0, 2).reshape(TOKENS, QHEADS * HEAD).astype(jnp.bfloat16)
    key_grad = lax.optimization_barrier(jnp.sum(key_parts.reshape(KVHEADS, group_size, TOKENS, HEAD), axis=1)).transpose(1, 0, 2).reshape(TOKENS, KVHEADS * HEAD).astype(jnp.bfloat16)
    value_grad = lax.optimization_barrier(jnp.sum(value_parts.reshape(KVHEADS, group_size, TOKENS, HEAD), axis=1)).transpose(1, 0, 2).reshape(TOKENS, KVHEADS * HEAD).astype(jnp.bfloat16)
    return (projected, query_grad, key_grad, value_grad)
```

```python
import math

import jax
import jax.numpy as jnp
from jax import lax
from jax.experimental import pallas as pl
from jax.experimental.pallas import tpu as pltpu
from jax.sharding import PartitionSpec as P

HEAD = 128
GROUP = 4
ROWS = 128
COLS = GROUP * HEAD
D = 8192
DOCS = 12
PART = 16
SLOTS = 9
NA = 4
AW = D // NA
NC = 8
CW = D // NC
SCALE = 1.0 / math.sqrt(HEAD)
MESH = pl.DeviceIdType.MESH
F32 = jnp.float32
BF16 = jnp.bfloat16


def dot(a, b, dims=((1,), (0,))):
    return lax.dot_general(a, b, (dims, ((), ())), preferred_element_type=F32)


def fold(a, op):
    return op(a.reshape(a.shape[0] // 8, 8, a.shape[1]), axis=0)


def kernel(
    docs_ref, q_hbm, k_hbm, v_hbm, w_hbm, g_hbm,
    proj_ref, dq_ref, dk_ref, dv_ref,
    w, g, q, qt, q4, kv, sc, pr, mx, ot, o, oz, zs, rz, tb, rl, xin,
    acc, do, dz, dost, dos4, dsb, dkv, ci, ri,
    lsem, wsem,
    agx_s, agx_r, agz_s, agz_r,
    kv_s, kv_r, kf_s,
    zh_s, zh_r,
    a_s, a_r, rl_s, rl_r, x_s, x_r,
    ci_s, ci_r, ri_s, ri_r,
):
    s, t = lax.axis_index("seq"), lax.axis_index("tensor")
    c, chip = s % 2, s // 2
    zh = chip % 2
    zl, x = t // 4, t % 4
    sz = s + 2 - 4 * zh
    tz = t + 4 - 8 * zl

    def at(seq, tensor):
        return {"seq": seq, "tensor": tensor}

    xr, xl = at(s, zl * 4 + (x + 1) % 4), at(s, zl * 4 + (x + 3) % 4)
    zp, zq, zhp = at(s, tz), at(sz, tz), at(sz, t)
    core = at(s + 1 - 2 * c, t)

    def chip_at(offset):
        return at(((chip + offset) % 8) * 2 + c, t)

    sent = []

    def send(src, dst, ss, rs, dev):
        copy = pltpu.make_async_remote_copy(
            src_ref=src, dst_ref=dst, send_sem=ss, recv_sem=rs, device_id=dev, device_id_type=MESH
        )
        copy.start()
        return copy

    def keep(*args):
        sent.append(send(*args))

    def arrived(dst, rs, dev, ss):
        pltpu.make_async_remote_copy(
            src_ref=dst, dst_ref=dst, send_sem=ss, recv_sem=rs, device_id=dev, device_id_type=MESH
        ).wait_recv()

    def block(pos):
        return pl.ds(pl.multiple_of(pos * PART, PART), PART)

    left, right, opp = (x + 3) % 4, (x + 1) % 4, (x + 2) % 4

    load_k = pltpu.make_async_copy(k_hbm, kv.at[0:ROWS, 0:HEAD], lsem.at[0])
    load_v = pltpu.make_async_copy(v_hbm, kv.at[0:ROWS, HEAD : 2 * HEAD], lsem.at[1])
    load_g = pltpu.make_async_copy(g_hbm, g.at[block(x), :], lsem.at[2])
    load_q = pltpu.make_async_copy(q_hbm, q, lsem.at[3])
    load_w = [
        pltpu.make_async_copy(w_hbm.at[:, k * CW : (k + 1) * CW], w.at[:, k * CW : (k + 1) * CW], wsem.at[k])
        for k in range(NC)
    ]
    for copy in [load_k, load_v, load_g, load_q] + load_w:
        copy.start()

    barrier = pltpu.get_barrier_semaphore()
    friends = [xr, xl, zp, zq, core] + [chip_at(j) for j in range(1, 8)]
    for dev in friends:
        pl.semaphore_signal(barrier, inc=1, device_id=dev, device_id_type=MESH)
    load_k.wait()
    load_v.wait()
    load_g.wait()
    pl.semaphore_wait(barrier, len(friends))

    def slot(d):
        return pl.ds(pl.multiple_of(d * ROWS, ROWS), ROWS)

    def forward(i):
        return pltpu.make_async_remote_copy(
            src_ref=kv.at[slot(2 * (i + c)), :],
            dst_ref=kv.at[slot(2 * i + 1), :],
            send_sem=kf_s.at[i],
            recv_sem=kv_r.at[2 * i + 1],
            device_id=core,
            device_id_type=MESH,
        )

    for hop in range(1, 5):
        keep(kv.at[0:ROWS, :], kv.at[slot(2 * hop), :], kv_s.at[hop - 1], kv_r.at[2 * hop], chip_at(hop))

    @pl.when(c == 0)
    def _():
        forward(0).start()

    def acols(a):
        return pl.ds(a * AW, AW)

    def to_z(pos, a, n):
        keep(
            g.at[block(pos), acols(a)],
            g.at[pl.ds(pl.multiple_of(64 + pos * PART, PART), PART), acols(a)],
            agz_s.at[n, a],
            agz_r.at[pos, a],
            at(s + (pos // 2) * (2 - 4 * zh), tz),
        )

    for a in range(NA):
        keep(g.at[block(x), acols(a)], g.at[block(x), acols(a)], agx_s.at[0, a], agx_r.at[0, a], xr)
        keep(g.at[block(x), acols(a)], g.at[block(x), acols(a)], agx_s.at[1, a], agx_r.at[1, a], xl)
        to_z(x, a, 0)

    def ag_near(a):
        arrived(g.at[block(left), acols(a)], agx_r.at[0, a], xr, agx_s.at[0, a])
        if a % 2 == 0:
            keep(g.at[block(left), acols(a)], g.at[block(left), acols(a)], agx_s.at[2, a], agx_r.at[2, a], xr)
        to_z(left, a, 1)
        arrived(g.at[block(right), acols(a)], agx_r.at[1, a], xl, agx_s.at[1, a])
        if a % 2 == 1:
            keep(g.at[block(right), acols(a)], g.at[block(right), acols(a)], agx_s.at[2, a], agx_r.at[2, a], xl)
        to_z(right, a, 2)

    def ag_far(a):
        arrived(g.at[block(opp), acols(a)], agx_r.at[2, a], xr, agx_s.at[2, a])
        to_z(opp, a, 3)

    load_q.wait()
    for h in range(GROUP):
        part = q[:, h * HEAD : (h + 1) * HEAD]
        q4[h * HEAD : (h + 1) * HEAD, :] = part
        qt[:, h * HEAD : (h + 1) * HEAD] = part.T

    own_pos = lax.broadcasted_iota(jnp.int32, (1, ROWS), 1) + s * ROWS
    start = jnp.zeros((1, ROWS), jnp.int32)
    end = jnp.int32(0)
    for j in range(DOCS):
        end = end + docs_ref[j]
        start = jnp.where(end <= own_pos, jnp.maximum(start, end), start)
    start = jnp.concatenate([start] * GROUP, axis=1)
    key_row = lax.broadcasted_iota(jnp.int32, (ROWS, COLS), 0)
    query_row = lax.broadcasted_iota(jnp.int32, (ROWS, COLS), 1) % ROWS

    def scores(d):
        st = dot(kv[d * ROWS : (d + 1) * ROWS, 0:HEAD], qt[...]) * SCALE
        seen = key_row >= start - (s - d) * ROWS
        if d == 0:
            seen = seen & (key_row <= query_row)
        st = jnp.where(seen, st, -1e30)
        sc[d * ROWS : (d + 1) * ROWS, :] = st
        top = fold(st, jnp.max)
        mx[...] = top if d == 0 else jnp.maximum(mx[...], top)

    scores(0)
    for a in range(NA):
        ag_near(a)
        hop = a + 1
        arrived(kv.at[slot(2 * hop), :], kv_r.at[2 * hop], core, kv_s.at[hop - 1])
        if hop < 4:
            forward(hop - c).start()
        else:

            @pl.when(c == 1)
            def _():
                forward(3).start()

        scores(2 * hop)
    for i in range(4):
        ag_far(i)
        arrived(kv.at[slot(2 * i + 1), :], kv_r.at[2 * i + 1], core, kf_s.at[i])
        scores(2 * i + 1)

    peak = jnp.max(mx[...], axis=0, keepdims=True)

    def weigh(d, total):
        p = jnp.exp(sc[slot(d), :] - peak)
        pr[slot(d), :] = p.astype(BF16)
        return total + fold(p, jnp.sum)

    total = lax.fori_loop(0, SLOTS, weigh, jnp.zeros((8, COLS), F32))
    inv = 1.0 / jnp.sum(total, axis=0, keepdims=True)
    ot[...] = dot(kv[:, HEAD : 2 * HEAD], pr[...], ((0,), (0,))) * inv
    for h in range(GROUP):
        o[:, h * HEAD : (h + 1) * HEAD] = ot[:, h * HEAD : (h + 1) * HEAD].T.astype(BF16)

    def orow(base, n):
        return pl.ds(pl.multiple_of(base, 32), n)

    keep(o.at[orow(64 * (1 - zl) + 32, 32), :], oz.at[32:64, :], zh_s.at[0], zh_r.at[0], zhp)
    oz[0:32, :] = o[orow(64 * (1 - zl), 32), :]

    def ccols(k):
        return pl.ds(k * CW, CW)

    for k in range(NC):
        load_w[k].wait()

    def wcols(k):
        return pl.ds(pl.multiple_of(k * CW, CW), CW)

    mine = o[orow(64 * zl, 64), :]

    @pl.loop(0, NC)
    def _(k):
        tb[:, wcols(k)] = dot(mine, w[:, wcols(k)]).astype(BF16)

    arrived(oz.at[32:64, :], zh_r.at[0], zhp, zh_s.at[0])
    for k in range(NC):
        zs[:, ccols(k)] = dot(oz[...], w[:, ccols(k)]).astype(BF16)
        keep(zs.at[0:32, ccols(k)], rz.at[0:32, ccols(k)], a_s.at[0, k], a_r.at[0, k], zp)
        keep(zs.at[32:64, ccols(k)], rz.at[32:64, ccols(k)], a_s.at[1, k], a_r.at[1, k], zq)

    for a in range(NA):
        for pos in range(4):
            arrived(
                g.at[64 + pos * PART : 64 + (pos + 1) * PART, acols(a)], agz_r.at[pos, a], zp, agz_s.at[0, a]
            )
        part = dot(g[:, acols(a)], w[:, acols(a)], ((1,), (1,)))
        acc[...] = part if a == 0 else acc[...] + part
    dz[...] = acc[96:128, :].astype(BF16)
    far = orow(64 * (1 - zl) + 32, 32)
    keep(dz, do.at[far, :], zh_s.at[1], zh_r.at[1], zhp)
    do[orow(64 * zl, 64), :] = acc[0:64, :].astype(BF16)
    do[orow(64 * (1 - zl), 32), :] = acc[64:96, :].astype(BF16)

    def near(k):
        arrived(rz.at[0:32, ccols(k)], a_r.at[0, k], zp, a_s.at[0, k])
        arrived(rz.at[32:64, ccols(k)], a_r.at[1, k], zq, a_s.at[1, k])
        tb[:, ccols(k)] = (tb[:, ccols(k)].astype(F32) + rz[:, ccols(k)].astype(F32)).astype(BF16)
        if k % 2 == 0:
            keep(tb.at[block(opp), ccols(k)], rl.at[:, ccols(k)], rl_s.at[k], rl_r.at[k], xr)
            keep(tb.at[block(left), ccols(k)], xin.at[1, :, ccols(k)], x_s.at[1, k], x_r.at[1, k], xl)
        else:
            keep(tb.at[block(opp), ccols(k)], rl.at[:, ccols(k)], rl_s.at[k], rl_r.at[k], xl)
            keep(tb.at[block(right), ccols(k)], xin.at[0, :, ccols(k)], x_s.at[0, k], x_r.at[0, k], xr)

    def relay(k):
        arrived(rl.at[:, ccols(k)], rl_r.at[k], xr, rl_s.at[k])
        to = right if k % 2 == 0 else left
        tb[block(to), ccols(k)] = (
            tb[block(to), ccols(k)].astype(F32) + rl[:, ccols(k)].astype(F32)
        ).astype(BF16)
        if k % 2 == 0:
            keep(tb.at[block(to), ccols(k)], xin.at[0, :, ccols(k)], x_s.at[0, k], x_r.at[0, k], xr)
        else:
            keep(tb.at[block(to), ccols(k)], xin.at[1, :, ccols(k)], x_s.at[1, k], x_r.at[1, k], xl)

    def finish(k):
        arrived(xin.at[0, :, ccols(k)], x_r.at[0, k], xr, x_s.at[0, k])
        arrived(xin.at[1, :, ccols(k)], x_r.at[1, k], xl, x_s.at[1, k])
        proj_ref[:, ccols(k)] = (
            tb[block(x), ccols(k)].astype(F32)
            + xin[0, :, ccols(k)].astype(F32)
            + xin[1, :, ccols(k)].astype(F32)
        ).astype(BF16)

    def prepare():
        arrived(do.at[far, :], zh_r.at[1], zhp, zh_s.at[1])
        for h in range(GROUP):
            cols = slice(h * HEAD, (h + 1) * HEAD)
            part = (do[:, cols].astype(F32).T * inv[:, cols]).astype(BF16)
            dost[:, cols] = part
            dos4[cols, :] = part.T
        return jnp.sum(dost[...].astype(F32) * ot[...], axis=0, keepdims=True)

    def back(d, delta):
        rows = slice(d * ROWS, (d + 1) * ROWS)
        slope = dot(kv[rows, HEAD : 2 * HEAD], dost[...])
        p = pr[rows, :]
        ds = (p.astype(F32) * (slope - delta)).astype(BF16)
        dsb[rows, :] = ds
        return dot(ds, q4[...]) * SCALE, dot(p, dos4[...])

    def back_odd(d, delta):
        i = d // 2
        dk, dv = back(d, delta)
        rows = slice(d * ROWS, (d + 1) * ROWS)
        dkv[rows, 0:HEAD] = dk.astype(BF16)
        dkv[rows, HEAD : 2 * HEAD] = dv.astype(BF16)
        keep(dkv.at[rows, :], ci.at[i], ci_s.at[i], ci_r.at[i], core)

    def add_core(i, d):
        arrived(ci.at[i], ci_r.at[i], core, ci_s.at[i])
        rows = slice(d * ROWS, (d + 1) * ROWS)
        dkv[rows, :] = (dkv[rows, :].astype(F32) + ci[i].astype(F32)).astype(BF16)

    def back_even(d, delta):
        hop = d // 2
        dk, dv = back(d, delta)
        rows = slice(d * ROWS, (d + 1) * ROWS)
        dkv[rows, 0:HEAD] = dk.astype(BF16)
        dkv[rows, HEAD : 2 * HEAD] = dv.astype(BF16)
        if hop == 4:
            pl.when(c == 1)(lambda: add_core(3, d))
        elif hop == 0:
            pl.when(c == 0)(lambda: add_core(0, d))
        else:
            add_core(hop - c, d)
        if hop > 0:
            keep(dkv.at[rows, :], ri.at[hop - 1], ri_s.at[hop - 1], ri_r.at[hop - 1], chip_at(8 - hop))

    near(0)
    near(1)
    delta = prepare()
    for d in (7, 5, 3, 1):
        back_odd(d, delta)
    relay(0)
    relay(1)
    back_even(8, delta)
    back_even(6, delta)
    near(2)
    relay(2)
    back_even(4, delta)
    back_even(2, delta)
    near(3)
    relay(3)
    back_even(0, delta)
    dqt = dot(kv[:, 0:HEAD], dsb[...], ((0,), (0,))) * SCALE
    for h in range(GROUP):
        cols = slice(h * HEAD, (h + 1) * HEAD)
        dq_ref[:, cols] = dqt[:, cols].T.astype(BF16)
    for k in range(4, NC):
        near(k)
        relay(k)
        finish(k - 4)
    for k in range(NC - 4, NC):
        finish(k)

    grad = dkv[0:ROWS, :].astype(F32)
    for i in range(4):
        arrived(ri.at[i], ri_r.at[i], core, ri_s.at[i])
        grad = grad + ri[i].astype(F32)
    dk_ref[...] = grad[:, 0:HEAD].astype(BF16)
    dv_ref[...] = grad[:, HEAD : 2 * HEAD].astype(BF16)

    for copy in sent:
        copy.wait_send()
    for i in range(4):
        forward(i).wait_send()


def body(queries, key_rows, values, out_weight, out_grad, doc_lengths):
    any_spec = pl.BlockSpec(memory_space=pl.ANY)
    vmem = pl.BlockSpec(memory_space=pltpu.VMEM)
    dma = pltpu.SemaphoreType.DMA
    scratch = [
        pltpu.VMEM((COLS, D), BF16),
        pltpu.VMEM((ROWS, D), BF16),
        pltpu.VMEM((ROWS, COLS), BF16),
        pltpu.VMEM((HEAD, COLS), BF16),
        pltpu.VMEM((COLS, HEAD), BF16),
        pltpu.VMEM((SLOTS * ROWS, 2 * HEAD), BF16),
        pltpu.VMEM((SLOTS * ROWS, COLS), F32),
        pltpu.VMEM((SLOTS * ROWS, COLS), BF16),
        pltpu.VMEM((8, COLS), F32),
        pltpu.VMEM((HEAD, COLS), F32),
        pltpu.VMEM((ROWS, COLS), BF16),
        pltpu.VMEM((64, COLS), BF16),
        pltpu.VMEM((64, D), BF16),
        pltpu.VMEM((64, D), BF16),
        pltpu.VMEM((64, D), BF16),
        pltpu.VMEM((PART, D), BF16),
        pltpu.VMEM((2, PART, D), BF16),
        pltpu.VMEM((ROWS, COLS), F32),
        pltpu.VMEM((ROWS, COLS), BF16),
        pltpu.VMEM((32, COLS), BF16),
        pltpu.VMEM((HEAD, COLS), BF16),
        pltpu.VMEM((COLS, HEAD), BF16),
        pltpu.VMEM((SLOTS * ROWS, COLS), BF16),
        pltpu.VMEM((SLOTS * ROWS, 2 * HEAD), BF16),
        pltpu.VMEM((4, ROWS, 2 * HEAD), BF16),
        pltpu.VMEM((4, ROWS, 2 * HEAD), BF16),
        dma((4,)), dma((NC,)),
        dma((3, NA)), dma((3, NA)), dma((4, NA)), dma((4, NA)),
        dma((4,)), dma((SLOTS,)), dma((4,)),
        dma((2,)), dma((2,)),
        dma((2, NC)), dma((2, NC)), dma((NC,)), dma((NC,)), dma((2, NC)), dma((2, NC)),
        dma((4,)), dma((4,)), dma((4,)), dma((4,)),
    ]
    return pl.pallas_call(
        kernel,
        out_shape=(
            jax.ShapeDtypeStruct((PART, D), BF16),
            jax.ShapeDtypeStruct((ROWS, COLS), BF16),
            jax.ShapeDtypeStruct((ROWS, HEAD), BF16),
            jax.ShapeDtypeStruct((ROWS, HEAD), BF16),
        ),
        in_specs=[pl.BlockSpec(memory_space=pltpu.SMEM)] + [any_spec] * 5,
        out_specs=(vmem,) * 4,
        scratch_shapes=scratch,
        compiler_params=pltpu.CompilerParams(
            collective_id=0, has_side_effects=True, vmem_limit_bytes=48 * 1024 * 1024
        ),
    )(doc_lengths, queries, key_rows, values, out_weight, out_grad)


def solution(mesh):
    return jax.shard_map(
        body,
        mesh=mesh,
        in_specs=(
            P("seq", "tensor"),
            P("seq", "tensor"),
            P("seq", "tensor"),
            P("tensor", None),
            P(("seq", "tensor"), None),
            P(),
        ),
        out_specs=(
            P(("seq", "tensor"), None),
            P("seq", "tensor"),
            P("seq", "tensor"),
            P("seq", "tensor"),
        ),
        check_vma=False,
    )
```

```python
import math

import jax
import jax.numpy as jnp
from jax import lax
from jax.experimental import pallas as pl
from jax.experimental.pallas import tpu as pltpu
from jax.sharding import PartitionSpec as P

HEAD = 128
GROUP = 4
ROWS = 128
COLS = GROUP * HEAD
D = 8192
DOCS = 12
PART = 16
SLOTS = 9
NA = 8
AW = D // NA
NC = 8
CW = D // NC
SCALE = 1.0 / math.sqrt(HEAD)
MESH = pl.DeviceIdType.MESH
F32 = jnp.float32
BF16 = jnp.bfloat16


def dot(a, b, dims=((1,), (0,))):
    return lax.dot_general(a, b, (dims, ((), ())), preferred_element_type=F32)


def fold(a, op):
    return op(a.reshape(a.shape[0] // 8, 8, a.shape[1]), axis=0)


def kernel(
    docs_hbm, q_hbm, k_hbm, v_hbm, w_hbm, g_hbm,
    proj_ref, dq_ref, dk_ref, dv_ref,
    docs_ref, w, g, q, qt, q4, kv, sc, pr, mx, ot, o, oz, zs, rz, tb, xin,
    acc, do, dz, dost, dos4, dsb, dkv, ci, ri,
    lsem, wsem,
    agx_s, agx_r, agz_s, agz_r,
    kv_s, kv_r, kf_s,
    zh_s, zh_r,
    a_s, a_r, x_s, x_r,
    ci_s, ci_r, ri_s, ri_r,
):
    s, t = lax.axis_index("seq"), lax.axis_index("tensor")
    c, chip = s % 2, s // 2
    zh = chip % 2
    zl, x = t // 4, t % 4
    sz = s + 2 - 4 * zh
    tz = t + 4 - 8 * zl

    def at(seq, tensor):
        return {"seq": seq, "tensor": tensor}

    beside = [at(s, zl * 4 + (x + j) % 4) for j in range(4)]
    zp, zq, zhp = at(s, tz), at(sz, tz), at(sz, t)
    core = at(s + 1 - 2 * c, t)

    def chip_at(offset):
        return at(((chip + offset) % 8) * 2 + c, t)

    sent = []

    def send(src, dst, ss, rs, dev):
        copy = pltpu.make_async_remote_copy(
            src_ref=src, dst_ref=dst, send_sem=ss, recv_sem=rs, device_id=dev, device_id_type=MESH
        )
        copy.start()
        return copy

    def keep(*args):
        sent.append(send(*args))

    def arrived(dst, rs, dev, ss):
        pltpu.make_async_remote_copy(
            src_ref=dst, dst_ref=dst, send_sem=ss, recv_sem=rs, device_id=dev, device_id_type=MESH
        ).wait_recv()

    def block(pos):
        return pl.ds(pl.multiple_of(pos * PART, PART), PART)

    left, right, opp = (x + 3) % 4, (x + 1) % 4, (x + 2) % 4

    barrier = pltpu.get_barrier_semaphore()
    friends = beside[1:] + [zp, zq, core] + [chip_at(j) for j in range(1, 8)]
    for dev in friends:
        pl.semaphore_signal(barrier, inc=1, device_id=dev, device_id_type=MESH)

    load_k = pltpu.make_async_copy(k_hbm, kv.at[0:ROWS, 0:HEAD], lsem.at[0])
    load_v = pltpu.make_async_copy(v_hbm, kv.at[0:ROWS, HEAD : 2 * HEAD], lsem.at[1])
    load_g = pltpu.make_async_copy(g_hbm, g.at[block(x), :], lsem.at[2])
    load_q = pltpu.make_async_copy(q_hbm, q, lsem.at[3])
    load_docs = pltpu.make_async_copy(docs_hbm, docs_ref, lsem.at[4])
    load_w = [
        pltpu.make_async_copy(w_hbm.at[:, k * CW : (k + 1) * CW], w.at[:, k * CW : (k + 1) * CW], wsem.at[k])
        for k in range(NC)
    ]
    for copy in [load_k, load_v, load_g, load_q, load_docs] + load_w:
        copy.start()

    load_k.wait()
    load_v.wait()
    load_g.wait()
    pl.semaphore_wait(barrier, len(friends))

    def slot(d):
        return pl.ds(pl.multiple_of(d * ROWS, ROWS), ROWS)

    def forward(i):
        return pltpu.make_async_remote_copy(
            src_ref=kv.at[slot(2 * (i + c)), :],
            dst_ref=kv.at[slot(2 * i + 1), :],
            send_sem=kf_s.at[i],
            recv_sem=kv_r.at[2 * i + 1],
            device_id=core,
            device_id_type=MESH,
        )

    for hop in range(1, 5):
        keep(kv.at[0:ROWS, :], kv.at[slot(2 * hop), :], kv_s.at[hop - 1], kv_r.at[2 * hop], chip_at(hop))

    @pl.when(c == 0)
    def _():
        forward(0).start()

    def acols(a):
        return pl.ds(a * AW, AW)

    def to_z(pos, a, n):
        keep(
            g.at[block(pos), acols(a)],
            g.at[pl.ds(pl.multiple_of(64 + pos * PART, PART), PART), acols(a)],
            agz_s.at[n, a],
            agz_r.at[pos, a],
            at(s + (pos // 2) * (2 - 4 * zh), tz),
        )

    for a in range(NA):
        for j in range(1, 4):
            keep(g.at[block(x), acols(a)], g.at[block(x), acols(a)], agx_s.at[j - 1, a], agx_r.at[j - 1, a], beside[j])
        to_z(x, a, 0)

    def ag_step(a):
        for j in (1, 3, 2):
            pos = (x + 4 - j) % 4
            arrived(g.at[block(pos), acols(a)], agx_r.at[j - 1, a], core, agx_s.at[j - 1, a])
            to_z(pos, a, j)

    load_q.wait()
    load_docs.wait()
    for h in range(GROUP):
        part = q[:, h * HEAD : (h + 1) * HEAD]
        q4[h * HEAD : (h + 1) * HEAD, :] = part
        qt[:, h * HEAD : (h + 1) * HEAD] = part.T

    own_pos = lax.broadcasted_iota(jnp.int32, (1, ROWS), 1) + s * ROWS
    start = jnp.zeros((1, ROWS), jnp.int32)
    end = jnp.int32(0)
    for j in range(DOCS):
        end = end + docs_ref[j]
        start = jnp.where(end <= own_pos, jnp.maximum(start, end), start)
    start = jnp.concatenate([start] * GROUP, axis=1)
    key_row = lax.broadcasted_iota(jnp.int32, (ROWS, COLS), 0)
    query_row = lax.broadcasted_iota(jnp.int32, (ROWS, COLS), 1) % ROWS

    def scores(d):
        st = dot(kv[d * ROWS : (d + 1) * ROWS, 0:HEAD], qt[...]) * SCALE
        seen = key_row >= start - (s - d) * ROWS
        if d == 0:
            seen = seen & (key_row <= query_row)
        st = jnp.where(seen, st, -1e30)
        sc[d * ROWS : (d + 1) * ROWS, :] = st
        top = fold(st, jnp.max)
        mx[...] = top if d == 0 else jnp.maximum(mx[...], top)

    def key_step(hop):
        arrived(kv.at[slot(2 * hop), :], kv_r.at[2 * hop], core, kv_s.at[hop - 1])
        if hop < 4:
            forward(hop - c).start()
        else:

            @pl.when(c == 1)
            def _():
                forward(3).start()

        scores(2 * hop)

    def odd_step(i):
        arrived(kv.at[slot(2 * i + 1), :], kv_r.at[2 * i + 1], core, kf_s.at[i])
        scores(2 * i + 1)

    scores(0)
    for hop in range(1, 5):
        key_step(hop)
        ag_step(hop - 1)
    for i in range(4):
        odd_step(i)

    peak = jnp.max(mx[...], axis=0, keepdims=True)

    def weigh(d, total):
        p = jnp.exp(sc[slot(d), :] - peak)
        pr[slot(d), :] = p.astype(BF16)
        return total + fold(p, jnp.sum)

    total = lax.fori_loop(0, SLOTS, weigh, jnp.zeros((8, COLS), F32))
    inv = 1.0 / jnp.sum(total, axis=0, keepdims=True)
    ot[...] = dot(kv[:, HEAD : 2 * HEAD], pr[...], ((0,), (0,))) * inv
    for h in range(GROUP):
        o[:, h * HEAD : (h + 1) * HEAD] = ot[:, h * HEAD : (h + 1) * HEAD].T.astype(BF16)

    def orow(base, n):
        return pl.ds(pl.multiple_of(base, 32), n)

    keep(o.at[orow(64 * (1 - zl) + 32, 32), :], oz.at[32:64, :], zh_s.at[0], zh_r.at[0], zhp)

    def ccols(k):
        return pl.ds(k * CW, CW)

    for k in range(NC):
        load_w[k].wait()

    def give(part, k):
        rows = slice(32 * part, 32 * part + 32)
        zs[rows, ccols(k)] = dot(oz[rows, :], w[:, ccols(k)]).astype(BF16)
        keep(
            zs.at[rows, ccols(k)], rz.at[rows, ccols(k)], a_s.at[part, k], a_r.at[part, k], zq if part else zp
        )

    mine = o[orow(64 * zl, 64), :]

    def own(k):
        tb[:, ccols(k)] = dot(mine, w[:, ccols(k)]).astype(BF16)

    oz[0:32, :] = o[orow(64 * (1 - zl), 32), :]
    ag_step(4)
    ag_step(5)
    for k in range(NC):
        give(0, k)
    ag_step(6)
    for k in range(NC):
        own(k)
    ag_step(7)
    arrived(oz.at[32:64, :], zh_r.at[0], zhp, zh_s.at[0])
    for k in range(NC):
        give(1, k)

    for a in range(NA):
        for pos in range(4):
            arrived(
                g.at[64 + pos * PART : 64 + (pos + 1) * PART, acols(a)], agz_r.at[pos, a], zp, agz_s.at[0, a]
            )
        part = dot(g[:, acols(a)], w[:, acols(a)], ((1,), (1,)))
        acc[...] = part if a == 0 else acc[...] + part
    dz[...] = acc[96:128, :].astype(BF16)
    far = orow(64 * (1 - zl) + 32, 32)
    keep(dz, do.at[far, :], zh_s.at[1], zh_r.at[1], zhp)
    do[orow(64 * zl, 64), :] = acc[0:64, :].astype(BF16)
    do[orow(64 * (1 - zl), 32), :] = acc[64:96, :].astype(BF16)

    def near(part, k):
        rows = slice(32 * part, 32 * part + 32)
        arrived(rz.at[rows, ccols(k)], a_r.at[part, k], zp, a_s.at[part, k])
        tb[rows, ccols(k)] = (tb[rows, ccols(k)].astype(F32) + rz[rows, ccols(k)].astype(F32)).astype(BF16)
        for to in (2 * part, 2 * part + 1):

            @pl.when(x != to)
            def _():
                x_copy(to, k).start()

    def x_copy(to, k):
        return pltpu.make_async_remote_copy(
            src_ref=tb.at[to * PART : (to + 1) * PART, ccols(k)],
            dst_ref=xin.at[x, :, ccols(k)],
            send_sem=x_s.at[to, k],
            recv_sem=x_r.at[x, k],
            device_id=at(s, zl * 4 + to),
            device_id_type=MESH,
        )

    def finish(k):
        total = tb[block(x), ccols(k)].astype(F32)
        for j in (1, 3, 2):
            pos = (x + j) % 4
            arrived(xin.at[pos, :, ccols(k)], x_r.at[pos, k], core, x_s.at[pos, k])
            total = total + xin[pos, :, ccols(k)].astype(F32)
        proj_ref[:, ccols(k)] = total.astype(BF16)

    def prepare():
        arrived(do.at[far, :], zh_r.at[1], zhp, zh_s.at[1])
        for h in range(GROUP):
            cols = slice(h * HEAD, (h + 1) * HEAD)
            part = (do[:, cols].astype(F32).T * inv[:, cols]).astype(BF16)
            dost[:, cols] = part
            dos4[cols, :] = part.T
        return jnp.sum(dost[...].astype(F32) * ot[...], axis=0, keepdims=True)

    def back(d, delta):
        rows = slice(d * ROWS, (d + 1) * ROWS)
        slope = dot(kv[rows, HEAD : 2 * HEAD], dost[...])
        p = pr[rows, :]
        ds = (p.astype(F32) * (slope - delta)).astype(BF16)
        dsb[rows, :] = ds
        return dot(ds, q4[...]) * SCALE, dot(p, dos4[...])

    def back_odd(d, delta):
        i = d // 2
        dk, dv = back(d, delta)
        rows = slice(d * ROWS, (d + 1) * ROWS)
        dkv[rows, 0:HEAD] = dk.astype(BF16)
        dkv[rows, HEAD : 2 * HEAD] = dv.astype(BF16)
        keep(dkv.at[rows, :], ci.at[i], ci_s.at[i], ci_r.at[i], core)

    def add_core(i, d):
        arrived(ci.at[i], ci_r.at[i], core, ci_s.at[i])
        rows = slice(d * ROWS, (d + 1) * ROWS)
        dkv[rows, :] = (dkv[rows, :].astype(F32) + ci[i].astype(F32)).astype(BF16)

    def back_even(d, delta):
        hop = d // 2
        dk, dv = back(d, delta)
        rows = slice(d * ROWS, (d + 1) * ROWS)
        dkv[rows, 0:HEAD] = dk.astype(BF16)
        dkv[rows, HEAD : 2 * HEAD] = dv.astype(BF16)
        if hop == 4:
            pl.when(c == 1)(lambda: add_core(3, d))
        elif hop == 0:
            pl.when(c == 0)(lambda: add_core(0, d))
        else:
            add_core(hop - c, d)
        if hop > 0:
            keep(dkv.at[rows, :], ri.at[hop - 1], ri_s.at[hop - 1], ri_r.at[hop - 1], chip_at(8 - hop))

    for k in range(4):
        near(0, k)
        near(1, k)
    delta = prepare()
    for d in (7, 5, 3, 1):
        back_odd(d, delta)
    for d in (8, 6, 4, 2):
        back_even(d, delta)
    for k in range(4, NC):
        near(0, k)
        near(1, k)
    back_even(0, delta)
    dqt = dot(kv[:, 0:HEAD], dsb[...], ((0,), (0,))) * SCALE
    for h in range(GROUP):
        cols = slice(h * HEAD, (h + 1) * HEAD)
        dq_ref[:, cols] = dqt[:, cols].T.astype(BF16)

    for copy in sent:
        copy.wait_send()
    for i in range(4):
        forward(i).wait_send()
    for to in range(4):

        @pl.when(x != to)
        def _():
            for k in range(NC):
                x_copy(to, k).wait_send()

    for k in range(NC):
        finish(k)

    grad = dkv[0:ROWS, :].astype(F32)
    for i in range(4):
        arrived(ri.at[i], ri_r.at[i], core, ri_s.at[i])
        grad = grad + ri[i].astype(F32)
    dk_ref[...] = grad[:, 0:HEAD].astype(BF16)
    dv_ref[...] = grad[:, HEAD : 2 * HEAD].astype(BF16)


def store(*refs):
    copies = [pltpu.make_async_copy(refs[i], refs[4 + i], refs[8].at[i]) for i in range(4)]
    for copy in copies:
        copy.start()
    for copy in copies:
        copy.wait()


def body(queries, key_rows, values, out_weight, out_grad, doc_lengths):
    hbm = pl.BlockSpec(memory_space=pltpu.HBM)
    vmem = pl.BlockSpec(memory_space=pltpu.VMEM)
    dma = pltpu.SemaphoreType.DMA
    scratch = [
        pltpu.SMEM((DOCS,), jnp.int32),
        pltpu.VMEM((COLS, D), BF16),
        pltpu.VMEM((ROWS, D), BF16),
        pltpu.VMEM((ROWS, COLS), BF16),
        pltpu.VMEM((HEAD, COLS), BF16),
        pltpu.VMEM((COLS, HEAD), BF16),
        pltpu.VMEM((SLOTS * ROWS, 2 * HEAD), BF16),
        pltpu.VMEM((SLOTS * ROWS, COLS), F32),
        pltpu.VMEM((SLOTS * ROWS, COLS), BF16),
        pltpu.VMEM((8, COLS), F32),
        pltpu.VMEM((HEAD, COLS), F32),
        pltpu.VMEM((ROWS, COLS), BF16),
        pltpu.VMEM((64, COLS), BF16),
        pltpu.VMEM((64, D), BF16),
        pltpu.VMEM((64, D), BF16),
        pltpu.VMEM((64, D), BF16),
        pltpu.VMEM((4, PART, D), BF16),
        pltpu.VMEM((ROWS, COLS), F32),
        pltpu.VMEM((ROWS, COLS), BF16),
        pltpu.VMEM((32, COLS), BF16),
        pltpu.VMEM((HEAD, COLS), BF16),
        pltpu.VMEM((COLS, HEAD), BF16),
        pltpu.VMEM((SLOTS * ROWS, COLS), BF16),
        pltpu.VMEM((SLOTS * ROWS, 2 * HEAD), BF16),
        pltpu.VMEM((4, ROWS, 2 * HEAD), BF16),
        pltpu.VMEM((4, ROWS, 2 * HEAD), BF16),
        dma((5,)), dma((NC,)),
        dma((3, NA)), dma((3, NA)), dma((4, NA)), dma((4, NA)),
        dma((4,)), dma((SLOTS,)), dma((4,)),
        dma((2,)), dma((2,)),
        dma((2, NC)), dma((2, NC)), dma((4, NC)), dma((4, NC)),
        dma((4,)), dma((4,)), dma((4,)), dma((4,)),
    ]
    shapes = (
        jax.ShapeDtypeStruct((PART, D), BF16),
        jax.ShapeDtypeStruct((ROWS, COLS), BF16),
        jax.ShapeDtypeStruct((ROWS, HEAD), BF16),
        jax.ShapeDtypeStruct((ROWS, HEAD), BF16),
    )
    results = pl.pallas_call(
        kernel,
        out_shape=shapes,
        in_specs=[hbm] * 6,
        out_specs=(vmem,) * 4,
        scratch_shapes=scratch,
        compiler_params=pltpu.CompilerParams(
            collective_id=0, has_side_effects=True, vmem_limit_bytes=63 * 1024 * 1024
        ),
    )(doc_lengths, queries, key_rows, values, out_weight, out_grad)
    return pl.pallas_call(
        store,
        out_shape=shapes,
        in_specs=[vmem] * 4,
        out_specs=(hbm,) * 4,
        scratch_shapes=[dma((4,))],
    )(*results)


def solution(mesh):
    return jax.shard_map(
        body,
        mesh=mesh,
        in_specs=(
            P("seq", "tensor"),
            P("seq", "tensor"),
            P("seq", "tensor"),
            P("tensor", None),
            P(("seq", "tensor"), None),
            P(),
        ),
        out_specs=(
            P(("seq", "tensor"), None),
            P("seq", "tensor"),
            P("seq", "tensor"),
            P("seq", "tensor"),
        ),
        check_vma=False,
    )
```

```python
import math

import jax
import jax.numpy as jnp
from jax import lax
from jax.experimental import pallas as pl
from jax.experimental.pallas import tpu as pltpu
from jax.sharding import PartitionSpec as P

HEAD = 128
GROUP = 4
ROWS = 128
COLS = GROUP * HEAD
D = 8192
DOCS = 12
PART = 16
SLOTS = 9
NA = 4
AW = D // NA
NC = 4
XFIRST = (0,)
CW = D // NC
SCALE = 1.0 / math.sqrt(HEAD)
MESH = pl.DeviceIdType.MESH
F32 = jnp.float32
BF16 = jnp.bfloat16


def dot(a, b, dims=((1,), (0,))):
    return lax.dot_general(a, b, (dims, ((), ())), preferred_element_type=F32)


def fold(a, op):
    return op(a.reshape(a.shape[0] // 8, 8, a.shape[1]), axis=0)


def kernel(
    docs_hbm, q_hbm, k_hbm, v_hbm, w_hbm, g_hbm,
    proj_ref, dq_ref, dk_ref, dv_ref,
    docs_ref, w, g, q, qt, q4, kv, sc, pr, mx, ot, o, oz, zs, rz, tb, xin, yin, ym, zin,
    acc, do, dz, dost, dos4, dsb, dkv, ci, fi, ri, rj, st,
    lsem, wsem,
    agx_s, agx_r, agz_s, agz_r,
    kv_s, kv_r, kf_s,
    zh_s, zh_r,
    a_s, a_r, x_s, x_r, y_s, y_r, m_s, m_r,
    ci_s, ci_r, fi_s, fi_r, ri_s, ri_r, rj_s, rj_r,
):
    s, t = lax.axis_index("seq"), lax.axis_index("tensor")
    c, chip = s % 2, s // 2
    zh = chip % 2
    zl, x = t // 4, t % 4
    sz = s + 2 - 4 * zh
    tz = t + 4 - 8 * zl

    def at(seq, tensor):
        return {"seq": seq, "tensor": tensor}

    beside = [at(s, zl * 4 + (x + j) % 4) for j in range(4)]
    zp, zq, zhp = at(s, tz), at(sz, tz), at(sz, t)
    core = at(s + 1 - 2 * c, t)

    def chip_at(offset):
        return at(((chip + offset) % 8) * 2 + c, t)

    sent = []

    def send(src, dst, ss, rs, dev):
        copy = pltpu.make_async_remote_copy(
            src_ref=src, dst_ref=dst, send_sem=ss, recv_sem=rs, device_id=dev, device_id_type=MESH
        )
        copy.start()
        return copy

    def keep(*args):
        sent.append(send(*args))

    def arrived(dst, rs, dev, ss):
        pltpu.make_async_remote_copy(
            src_ref=dst, dst_ref=dst, send_sem=ss, recv_sem=rs, device_id=dev, device_id_type=MESH
        ).wait_recv()

    def block(pos):
        return pl.ds(pl.multiple_of(pos * PART, PART), PART)

    left, right, opp = (x + 3) % 4, (x + 1) % 4, (x + 2) % 4

    barrier = pltpu.get_barrier_semaphore()
    friends = beside[1:] + [zp, zq, zhp, core] + [chip_at(j) for j in (2, 4, 6)]
    for dev in friends:
        pl.semaphore_signal(barrier, inc=1, device_id=dev, device_id_type=MESH)

    load_k = pltpu.make_async_copy(k_hbm, kv.at[0:ROWS, 0:HEAD], lsem.at[0])
    load_v = pltpu.make_async_copy(v_hbm, kv.at[0:ROWS, HEAD : 2 * HEAD], lsem.at[1])
    load_g = pltpu.make_async_copy(g_hbm, g.at[block(x), :], lsem.at[2])
    load_q = pltpu.make_async_copy(q_hbm, q, lsem.at[3])
    load_docs = pltpu.make_async_copy(docs_hbm, docs_ref, lsem.at[4])
    load_w = [
        pltpu.make_async_copy(w_hbm.at[:, k * CW : (k + 1) * CW], w.at[:, k * CW : (k + 1) * CW], wsem.at[k])
        for k in range(NC)
    ]
    for copy in [load_k, load_v, load_g, load_q, load_docs] + load_w:
        copy.start()

    load_k.wait()
    load_v.wait()
    load_g.wait()
    pl.semaphore_wait(barrier, len(friends))

    def slot(d):
        return pl.ds(pl.multiple_of(d * ROWS, ROWS), ROWS)

    def forward(i):
        return pltpu.make_async_remote_copy(
            src_ref=kv.at[slot(2 * (i + c)), :],
            dst_ref=kv.at[slot(2 * i + 1), :],
            send_sem=kf_s.at[i],
            recv_sem=kv_r.at[2 * i + 1],
            device_id=core,
            device_id_type=MESH,
        )

    def flip():
        return pltpu.make_async_remote_copy(
            src_ref=kv.at[0:ROWS, :],
            dst_ref=kv.at[slot(2 + 7 * zh), :],
            send_sem=kv_s.at[2],
            recv_sem=kv_r.at[2 + 7 * zh],
            device_id=zhp,
            device_id_type=MESH,
        )

    def pass_on(i):
        return pltpu.make_async_remote_copy(
            src_ref=kv.at[slot(9 - 7 * zh), :],
            dst_ref=kv.at[slot(6 if i else 2 + 4 * zh), :],
            send_sem=kv_s.at[3 + i],
            recv_sem=kv_r.at[6 if i else 2 + 4 * zh],
            device_id=chip_at(4 if i else 2),
            device_id_type=MESH,
        )

    flip().start()
    for i in range(2):
        keep(kv.at[0:ROWS, :], kv.at[slot(4 * i + 4), :], kv_s.at[i], kv_r.at[4 * i + 4], chip_at(2 * i + 2))

    @pl.when(c == 0)
    def _():
        forward(0).start()

    def orow(base, n):
        return pl.ds(pl.multiple_of(base, 32), n)

    far = orow(64 * (1 - zl) + 32, 32)

    def acols(a):
        return pl.ds(a * AW, AW)

    def to_z(pos, a, n):
        keep(
            g.at[block(pos), acols(a)],
            g.at[pl.ds(pl.multiple_of(64 + pos * PART, PART), PART), acols(a)],
            agz_s.at[n, a],
            agz_r.at[pos, a],
            at(s + (pos // 2) * (2 - 4 * zh), tz),
        )

    for a in range(NA):
        for j in range(1, 4):
            keep(g.at[block(x), acols(a)], g.at[block(x), acols(a)], agx_s.at[j - 1, a], agx_r.at[j - 1, a], beside[j])

    def ag_part(a, j):
        pos = (x + 4 - j) % 4
        arrived(g.at[block(pos), acols(a)], agx_r.at[j - 1, a], core, agx_s.at[j - 1, a])
        to_z(pos, a, j)

    def ag_step(a):
        for j in (1, 3, 2):
            ag_part(a, j)

    load_q.wait()
    load_docs.wait()
    for h in range(GROUP):
        part = q[:, h * HEAD : (h + 1) * HEAD]
        q4[h * HEAD : (h + 1) * HEAD, :] = part
        qt[:, h * HEAD : (h + 1) * HEAD] = part.T

    own_pos = lax.broadcasted_iota(jnp.int32, (1, ROWS), 1) + s * ROWS
    start = jnp.zeros((1, ROWS), jnp.int32)
    end = jnp.int32(0)
    for j in range(DOCS):
        end = end + docs_ref[j]
        start = jnp.where(end <= own_pos, jnp.maximum(start, end), start)
    start = jnp.concatenate([start] * GROUP, axis=1)
    key_row = lax.broadcasted_iota(jnp.int32, (ROWS, COLS), 0)
    query_row = lax.broadcasted_iota(jnp.int32, (ROWS, COLS), 1) % ROWS

    def scores(d):
        st = dot(kv[d * ROWS : (d + 1) * ROWS, 0:HEAD], qt[...]) * SCALE
        seen = key_row >= start - (s - d) * ROWS
        if d == 0:
            seen = seen & (key_row <= query_row)
        st = jnp.where(seen, st, -1e30)
        sc[d * ROWS : (d + 1) * ROWS, :] = st
        top = fold(st, jnp.max)
        mx[...] = top if d == 0 else jnp.maximum(mx[...], top)

    def flip_step():
        arrived(kv.at[slot(9 - 7 * zh), :], kv_r.at[9 - 7 * zh], core, kv_s.at[0])
        pass_on(0).start()

        @pl.when(zh == 0)
        def _():
            pass_on(1).start()

    def key_step(hop):
        if hop == 1:

            @pl.when(zh == 0)
            def _():
                arrived(kv.at[slot(2), :], kv_r.at[2], core, kv_s.at[0])
        else:
            arrived(kv.at[slot(2 * hop), :], kv_r.at[2 * hop], core, kv_s.at[0])
        if hop < 4:
            forward(hop - c).start()
        else:

            @pl.when(c == 1)
            def _():
                forward(3).start()

        scores(2 * hop)

    def odd_step(i):
        arrived(kv.at[slot(2 * i + 1), :], kv_r.at[2 * i + 1], core, kf_s.at[i])
        scores(2 * i + 1)

    def ccols(k):
        return pl.ds(k * CW, CW)

    given = {}

    def give(part, k):
        rows = slice(32 * part, 32 * part + 32)
        zs[rows, ccols(k)] = dot(oz[rows, :], w[:, ccols(k)]).astype(BF16)
        given[part, k] = send(
            zs.at[rows, ccols(k)], rz.at[rows, ccols(k)], a_s.at[part, k], a_r.at[part, k], zq if part else zp
        )

    def own(k):
        tb[:, ccols(k)] = dot(mine, w[:, ccols(k)]).astype(BF16)
        if k in XFIRST:
            for to in range(4):

                @pl.when(x != to)
                def _():
                    x_copy(to, k).start()

    def spread(part, k):
        rows = slice(32 * part, 32 * part + 32)
        zs[rows, ccols(k)] = dot(oz[rows, :], w[:, ccols(k)]).astype(BF16)
        for to in (2 * part, 2 * part + 1):

            @pl.when(x != to)
            def _():
                y_copy(to, k).start()

    def y_copy(to, k):
        return pltpu.make_async_remote_copy(
            src_ref=zs.at[to * PART : (to + 1) * PART, ccols(k)],
            dst_ref=yin.at[x, :, ccols(k)],
            send_sem=y_s.at[to, k],
            recv_sem=y_r.at[x, k],
            device_id=at(s, zl * 4 + to),
            device_id_type=MESH,
        )

    def middle(k):
        total = zs[block(x), ccols(k)].astype(F32)
        for j in (1, 3, 2):
            pos = (x + j) % 4
            arrived(yin.at[pos, :, ccols(k)], y_r.at[pos, k], core, y_s.at[pos, k])
            total = total + yin[pos, :, ccols(k)].astype(F32)
        ym[:, ccols(k)] = total.astype(BF16)
        keep(
            ym.at[:, ccols(k)], zin.at[:, ccols(k)], m_s.at[k], m_r.at[k], at(s + (x // 2) * (2 - 4 * zh), tz)
        )

    def attn_grad(a):
        for pos in range(4):
            arrived(
                g.at[64 + pos * PART : 64 + (pos + 1) * PART, acols(a)], agz_r.at[pos, a], zp, agz_s.at[0, a]
            )
        part = dot(g[:, acols(a)], w[:, acols(a)], ((1,), (1,)))
        acc[...] = part if a == 0 else acc[...] + part

    def near(part, k):
        rows = slice(32 * part, 32 * part + 32)
        arrived(rz.at[rows, ccols(k)], a_r.at[part, k], zp, a_s.at[part, k])
        tb[rows, ccols(k)] = (tb[rows, ccols(k)].astype(F32) + rz[rows, ccols(k)].astype(F32)).astype(BF16)
        for to in (2 * part, 2 * part + 1):

            @pl.when(x != to)
            def _():
                x_copy(to, k).start()

    def x_copy(to, k):
        return pltpu.make_async_remote_copy(
            src_ref=tb.at[to * PART : (to + 1) * PART, ccols(k)],
            dst_ref=xin.at[x, :, ccols(k)],
            send_sem=x_s.at[to, k],
            recv_sem=x_r.at[x, k],
            device_id=at(s, zl * 4 + to),
            device_id_type=MESH,
        )

    def finish(k):
        total = tb[block(x), ccols(k)].astype(F32)
        if k in XFIRST:
            arrived(zin.at[:, ccols(k)], m_r.at[k], core, m_s.at[k])
            total = total + zin[:, ccols(k)].astype(F32)
        for j in (1, 3, 2):
            pos = (x + j) % 4
            arrived(xin.at[pos, :, ccols(k)], x_r.at[pos, k], core, x_s.at[pos, k])
            total = total + xin[pos, :, ccols(k)].astype(F32)
        proj_ref[:, ccols(k)] = total.astype(BF16)

    def prepare():
        arrived(do.at[far, :], zh_r.at[1], zhp, zh_s.at[1])
        for h in range(GROUP):
            cols = slice(h * HEAD, (h + 1) * HEAD)
            part = (do[:, cols].astype(F32).T * inv[:, cols]).astype(BF16)
            dost[:, cols] = part
            dos4[cols, :] = part.T
        return jnp.sum(dost[...].astype(F32) * ot[...], axis=0, keepdims=True)

    def back(d, delta):
        rows = slice(d * ROWS, (d + 1) * ROWS)
        slope = dot(kv[rows, HEAD : 2 * HEAD], dost[...])
        p = pr[rows, :]
        ds = (p.astype(F32) * (slope - delta)).astype(BF16)
        dsb[rows, :] = ds
        return dot(ds, q4[...]) * SCALE, dot(p, dos4[...])

    def back_odd(d, delta):
        i = d // 2
        dk, dv = back(d, delta)
        rows = slice(d * ROWS, (d + 1) * ROWS)
        dkv[rows, 0:HEAD] = dk.astype(BF16)
        dkv[rows, HEAD : 2 * HEAD] = dv.astype(BF16)
        keep(dkv.at[rows, :], ci.at[i], ci_s.at[i], ci_r.at[i], core)

    def add_core(i, d):
        arrived(ci.at[i], ci_r.at[i], core, ci_s.at[i])
        rows = slice(d * ROWS, (d + 1) * ROWS)
        dkv[rows, :] = (dkv[rows, :].astype(F32) + ci[i].astype(F32)).astype(BF16)

    def back_even(d, delta):
        hop = d // 2
        dk, dv = back(d, delta)
        rows = slice(d * ROWS, (d + 1) * ROWS)
        dkv[rows, 0:HEAD] = dk.astype(BF16)
        dkv[rows, HEAD : 2 * HEAD] = dv.astype(BF16)
        if hop == 4:
            pl.when(c == 1)(lambda: add_core(3, d))
        elif hop == 0:
            pl.when(c == 0)(lambda: add_core(0, d))
        else:
            add_core(hop - c, d)
        if hop % 2 == 0 and hop > 0:
            i = hop // 2 - 1
            keep(dkv.at[rows, :], ri.at[i], ri_s.at[i], ri_r.at[i], chip_at(6 - 2 * i))

    def hand_back(i):
        return pltpu.make_async_remote_copy(
            src_ref=dkv.at[slot(6 if i else 2 + 4 * zh), :],
            dst_ref=rj.at[i],
            send_sem=rj_s.at[i],
            recv_sem=rj_r.at[i],
            device_id=chip_at(4 if i else 6),
            device_id_type=MESH,
        )

    def flip_back():
        arrived(rj.at[0], rj_r.at[0], core, rj_s.at[0])

        @pl.when(zh == 0)
        def _():
            arrived(rj.at[1], rj_r.at[1], core, rj_s.at[1])
            st[...] = (rj[0].astype(F32) + rj[1].astype(F32)).astype(BF16)

        @pl.when(zh == 1)
        def _():
            st[...] = (rj[0].astype(F32) + dkv[2 * ROWS : 3 * ROWS, :].astype(F32)).astype(BF16)

        keep(st, fi, fi_s.at[0], fi_r.at[0], zhp)

    for a in range(NA):
        to_z(x, a, 0)
    scores(0)
    flip_step()
    key_step(2)
    key_step(4)
    ag_step(0)
    ag_step(1)
    key_step(1)
    key_step(3)
    odd_step(1)
    odd_step(0)
    odd_step(3)
    odd_step(2)
    ag_step(2)
    peak = jnp.max(mx[...], axis=0, keepdims=True)

    def weigh(d, total):
        p = jnp.exp(sc[slot(d), :] - peak)
        pr[slot(d), :] = p.astype(BF16)
        return total + fold(p, jnp.sum)

    total = lax.fori_loop(0, SLOTS, weigh, jnp.zeros((8, COLS), F32))
    inv = 1.0 / jnp.sum(total, axis=0, keepdims=True)
    ot[...] = dot(kv[0 : SLOTS * ROWS, HEAD : 2 * HEAD], pr[...], ((0,), (0,))) * inv
    for h in range(GROUP):
        o[:, h * HEAD : (h + 1) * HEAD] = ot[:, h * HEAD : (h + 1) * HEAD].T.astype(BF16)

    keep(o.at[orow(64 * (1 - zl) + 32, 32), :], oz.at[32:64, :], zh_s.at[0], zh_r.at[0], zhp)

    for k in range(NC):
        load_w[k].wait()

    mine = o[orow(64 * zl, 64), :]

    oz[0:32, :] = o[orow(64 * (1 - zl), 32), :]
    ag_step(3)
    own(0)
    spread(0, 0)
    own(1)
    own(2)
    own(3)
    give(0, 1)
    arrived(oz.at[32:64, :], zh_r.at[0], zhp, zh_s.at[0])
    spread(1, 0)
    give(1, 1)
    attn_grad(0)
    attn_grad(1)
    attn_grad(2)
    attn_grad(3)
    dz[...] = acc[96:128, :].astype(BF16)
    keep(dz, do.at[far, :], zh_s.at[1], zh_r.at[1], zhp)
    do[orow(64 * zl, 64), :] = acc[0:64, :].astype(BF16)
    do[orow(64 * (1 - zl), 32), :] = acc[64:96, :].astype(BF16)
    give(0, 2)
    give(1, 2)
    give(0, 3)
    give(1, 3)
    middle(0)
    near(0, 1)
    near(1, 1)
    delta = prepare()
    back_odd(7, delta)
    back_odd(5, delta)
    back_odd(3, delta)
    back_odd(1, delta)
    back_even(6, delta)
    back_even(2, delta)
    hand_back(0).start()

    @pl.when(zh == 0)
    def _():
        hand_back(1).start()

    near(0, 2)
    back_even(8, delta)
    near(1, 2)
    back_even(4, delta)
    back_even(0, delta)
    near(0, 3)
    flip_back()
    near(1, 3)
    dqt = dot(kv[0 : SLOTS * ROWS, 0:HEAD], dsb[...], ((0,), (0,))) * SCALE
    for h in range(GROUP):
        cols = slice(h * HEAD, (h + 1) * HEAD)
        dq_ref[:, cols] = dqt[:, cols].T.astype(BF16)
    for copy in given.values():
        copy.wait_send()
    for copy in sent:
        copy.wait_send()
    for i in range(4):
        forward(i).wait_send()
    flip().wait_send()
    pass_on(0).wait_send()
    hand_back(0).wait_send()

    @pl.when(zh == 0)
    def _():
        pass_on(1).wait_send()
        hand_back(1).wait_send()

    for to in range(4):

        @pl.when(x != to)
        def _():
            for k in range(NC):
                x_copy(to, k).wait_send()
            for k in XFIRST:
                y_copy(to, k).wait_send()
    for k in range(NC):
        finish(k)

    grad = dkv[0:ROWS, :].astype(F32)
    arrived(fi, fi_r.at[0], zhp, fi_s.at[0])
    grad = grad + fi[...].astype(F32)
    for i in range(2):
        arrived(ri.at[i], ri_r.at[i], core, ri_s.at[i])
        grad = grad + ri[i].astype(F32)
    dk_ref[...] = grad[:, 0:HEAD].astype(BF16)
    dv_ref[...] = grad[:, HEAD : 2 * HEAD].astype(BF16)

def store(*refs):
    copies = [pltpu.make_async_copy(refs[i], refs[4 + i], refs[8].at[i]) for i in range(4)]
    for copy in copies:
        copy.start()
    for copy in copies:
        copy.wait()


def body(queries, key_rows, values, out_weight, out_grad, doc_lengths):
    hbm = pl.BlockSpec(memory_space=pltpu.HBM)
    vmem = pl.BlockSpec(memory_space=pltpu.VMEM)
    dma = pltpu.SemaphoreType.DMA
    scratch = [
        pltpu.SMEM((DOCS,), jnp.int32),
        pltpu.VMEM((COLS, D), BF16),
        pltpu.VMEM((ROWS, D), BF16),
        pltpu.VMEM((ROWS, COLS), BF16),
        pltpu.VMEM((HEAD, COLS), BF16),
        pltpu.VMEM((COLS, HEAD), BF16),
        pltpu.VMEM(((SLOTS + 1) * ROWS, 2 * HEAD), BF16),
        pltpu.VMEM((SLOTS * ROWS, COLS), F32),
        pltpu.VMEM((SLOTS * ROWS, COLS), BF16),
        pltpu.VMEM((8, COLS), F32),
        pltpu.VMEM((HEAD, COLS), F32),
        pltpu.VMEM((ROWS, COLS), BF16),
        pltpu.VMEM((64, COLS), BF16),
        pltpu.VMEM((64, D), BF16),
        pltpu.VMEM((64, D), BF16),
        pltpu.VMEM((64, D), BF16),
        pltpu.VMEM((4, PART, D), BF16),
        pltpu.VMEM((4, PART, D), BF16),
        pltpu.VMEM((PART, D), BF16),
        pltpu.VMEM((PART, D), BF16),
        pltpu.VMEM((ROWS, COLS), F32),
        pltpu.VMEM((ROWS, COLS), BF16),
        pltpu.VMEM((32, COLS), BF16),
        pltpu.VMEM((HEAD, COLS), BF16),
        pltpu.VMEM((COLS, HEAD), BF16),
        pltpu.VMEM((SLOTS * ROWS, COLS), BF16),
        pltpu.VMEM((SLOTS * ROWS, 2 * HEAD), BF16),
        pltpu.VMEM((4, ROWS, 2 * HEAD), BF16),
        pltpu.VMEM((ROWS, 2 * HEAD), BF16),
        pltpu.VMEM((2, ROWS, 2 * HEAD), BF16),
        pltpu.VMEM((2, ROWS, 2 * HEAD), BF16),
        pltpu.VMEM((ROWS, 2 * HEAD), BF16),
        dma((5,)), dma((NC,)),
        dma((3, NA)), dma((3, NA)), dma((4, NA)), dma((4, NA)),
        dma((5,)), dma((SLOTS + 1,)), dma((4,)),
        dma((2,)), dma((2,)),
        dma((2, NC)), dma((2, NC)), dma((4, NC)), dma((4, NC)),
        dma((4, NC)), dma((4, NC)), dma((NC,)), dma((NC,)),
        dma((4,)), dma((4,)), dma((1,)), dma((1,)), dma((2,)), dma((2,)), dma((2,)), dma((2,)),
    ]
    shapes = (
        jax.ShapeDtypeStruct((PART, D), BF16),
        jax.ShapeDtypeStruct((ROWS, COLS), BF16),
        jax.ShapeDtypeStruct((ROWS, HEAD), BF16),
        jax.ShapeDtypeStruct((ROWS, HEAD), BF16),
    )
    results = pl.pallas_call(
        kernel,
        out_shape=shapes,
        in_specs=[hbm] * 6,
        out_specs=(vmem,) * 4,
        scratch_shapes=scratch,
        compiler_params=pltpu.CompilerParams(
            collective_id=0, has_side_effects=True, vmem_limit_bytes=63 * 1024 * 1024
        ),
    )(doc_lengths, queries, key_rows, values, out_weight, out_grad)
    return pl.pallas_call(
        store,
        out_shape=shapes,
        in_specs=[vmem] * 4,
        out_specs=(hbm,) * 4,
        scratch_shapes=[dma((4,))],
    )(*results)


def solution(mesh):
    return jax.shard_map(
        body,
        mesh=mesh,
        in_specs=(
            P("seq", "tensor"),
            P("seq", "tensor"),
            P("seq", "tensor"),
            P("tensor", None),
            P(("seq", "tensor"), None),
            P(),
        ),
        out_specs=(
            P(("seq", "tensor"), None),
            P("seq", "tensor"),
            P("seq", "tensor"),
            P("seq", "tensor"),
        ),
        check_vma=False,
    )
```

```python
import math

import jax
import jax.numpy as jnp
from jax import lax
from jax.experimental import pallas as pl
from jax.experimental.pallas import tpu as pltpu
from jax.sharding import PartitionSpec as P

HEAD = 128
GROUP = 4
ROWS = 128
COLS = GROUP * HEAD
D = 8192
DOCS = 12
PART = 16
SLOTS = 9
NA = 4
AW = D // NA
NC = 4
XFIRST = (0,)
CW = D // NC
SCALE = 1.0 / math.sqrt(HEAD)
MESH = pl.DeviceIdType.MESH
F32 = jnp.float32
BF16 = jnp.bfloat16


def dot(a, b, dims=((1,), (0,))):
    return lax.dot_general(a, b, (dims, ((), ())), preferred_element_type=F32)


def fold(a, op):
    return op(a.reshape(a.shape[0] // 8, 8, a.shape[1]), axis=0)


def kernel(
    docs_hbm, q_hbm, k_hbm, v_hbm, w_hbm, g_hbm,
    proj_ref, dq_ref, dk_ref, dv_ref,
    docs_ref, w, g, q, qt, q4, kv, sc, pr, mx, ot, o, oz, zs, rz, tb, xin, yin, ym, zin,
    acc, do, dz, dost, dos4, dsb, dkv, ci, fi, ri, rj, st,
    lsem, wsem,
    agx_s, agx_r, agz_s, agz_r, zx_s, zx_r,
    kv_s, kv_r, kf_s,
    zh_s, zh_r,
    a_s, a_r, x_s, x_r, y_s, y_r, m_s, m_r,
    ci_s, ci_r, fi_s, fi_r, ri_s, ri_r, rj_s, rj_r,
):
    s, t = lax.axis_index("seq"), lax.axis_index("tensor")
    c, chip = s % 2, s // 2
    zh = chip % 2
    zl, x = t // 4, t % 4
    sz = s + 2 - 4 * zh
    tz = t + 4 - 8 * zl

    def at(seq, tensor):
        return {"seq": seq, "tensor": tensor}

    beside = [at(s, zl * 4 + (x + j) % 4) for j in range(4)]
    zp, zq, zhp = at(s, tz), at(sz, tz), at(sz, t)
    core = at(s + 1 - 2 * c, t)

    def chip_at(offset):
        return at(((chip + offset) % 8) * 2 + c, t)

    sent = []

    def send(src, dst, ss, rs, dev):
        copy = pltpu.make_async_remote_copy(
            src_ref=src, dst_ref=dst, send_sem=ss, recv_sem=rs, device_id=dev, device_id_type=MESH
        )
        copy.start()
        return copy

    def keep(*args):
        sent.append(send(*args))

    def arrived(dst, rs, dev, ss):
        pltpu.make_async_remote_copy(
            src_ref=dst, dst_ref=dst, send_sem=ss, recv_sem=rs, device_id=dev, device_id_type=MESH
        ).wait_recv()

    def block(pos):
        return pl.ds(pl.multiple_of(pos * PART, PART), PART)

    left, right, opp = (x + 3) % 4, (x + 1) % 4, (x + 2) % 4

    barrier = pltpu.get_barrier_semaphore()
    friends = beside[1:] + [zp, zq, zhp, core] + [chip_at(j) for j in (2, 4, 6)]
    for dev in friends:
        pl.semaphore_signal(barrier, inc=1, device_id=dev, device_id_type=MESH)

    load_k = pltpu.make_async_copy(k_hbm, kv.at[0:ROWS, 0:HEAD], lsem.at[0])
    load_v = pltpu.make_async_copy(v_hbm, kv.at[0:ROWS, HEAD : 2 * HEAD], lsem.at[1])
    load_g = pltpu.make_async_copy(g_hbm, g.at[block(x), :], lsem.at[2])
    load_q = pltpu.make_async_copy(q_hbm, q, lsem.at[3])
    load_docs = pltpu.make_async_copy(docs_hbm, docs_ref, lsem.at[4])
    load_w = [
        pltpu.make_async_copy(w_hbm.at[:, k * CW : (k + 1) * CW], w.at[:, k * CW : (k + 1) * CW], wsem.at[k])
        for k in range(NC)
    ]
    for copy in [load_k, load_v, load_g, load_q, load_docs] + load_w:
        copy.start()

    load_k.wait()
    load_v.wait()
    load_g.wait()
    pl.semaphore_wait(barrier, len(friends))

    def slot(d):
        return pl.ds(pl.multiple_of(d * ROWS, ROWS), ROWS)

    def forward(i):
        return pltpu.make_async_remote_copy(
            src_ref=kv.at[slot(2 * (i + c)), :],
            dst_ref=kv.at[slot(2 * i + 1), :],
            send_sem=kf_s.at[i],
            recv_sem=kv_r.at[2 * i + 1],
            device_id=core,
            device_id_type=MESH,
        )

    def flip():
        return pltpu.make_async_remote_copy(
            src_ref=kv.at[0:ROWS, :],
            dst_ref=kv.at[slot(2 + 7 * zh), :],
            send_sem=kv_s.at[2],
            recv_sem=kv_r.at[2 + 7 * zh],
            device_id=zhp,
            device_id_type=MESH,
        )

    def pass_on(i):
        return pltpu.make_async_remote_copy(
            src_ref=kv.at[slot(9 - 7 * zh), :],
            dst_ref=kv.at[slot(6 if i else 2 + 4 * zh), :],
            send_sem=kv_s.at[3 + i],
            recv_sem=kv_r.at[6 if i else 2 + 4 * zh],
            device_id=chip_at(4 if i else 2),
            device_id_type=MESH,
        )

    flip().start()
    for i in range(2):
        keep(kv.at[0:ROWS, :], kv.at[slot(4 * i + 4), :], kv_s.at[i], kv_r.at[4 * i + 4], chip_at(2 * i + 2))

    @pl.when(c == 0)
    def _():
        forward(0).start()

    def orow(base, n):
        return pl.ds(pl.multiple_of(base, 32), n)

    far = orow(64 * (1 - zl) + 32, 32)

    def acols(a):
        return pl.ds(a * AW, AW)

    def to_z(pos, a, n):
        keep(
            g.at[block(pos), acols(a)],
            g.at[pl.ds(pl.multiple_of(64 + pos * PART, PART), PART), acols(a)],
            agz_s.at[n, a],
            agz_r.at[pos, a],
            at(s + (pos // 2) * (2 - 4 * zh), tz),
        )

    for a in range(NA):
        for j in range(1, 4):
            keep(g.at[block(x), acols(a)], g.at[block(x), acols(a)], agx_s.at[j - 1, a], agx_r.at[j - 1, a], beside[j])

    def zblock(pos):
        return pl.ds(pl.multiple_of(64 + pos * PART, PART), PART)

    def z_first():
        last = NA - 1
        here = g.at[zblock(x), acols(last)]
        arrived(here, agz_r.at[x, last], zp, agz_s.at[0, last])
        for j in (1, 3, 2):
            keep(here, here, zx_s.at[j - 1], zx_r.at[j - 1], beside[j])

    def ag_last():
        last = NA - 1
        for j in (1, 3, 2):
            pos = (x + 4 - j) % 4
            arrived(g.at[block(pos), acols(last)], agx_r.at[j - 1, last], core, agx_s.at[j - 1, last])
            arrived(g.at[zblock(pos), acols(last)], zx_r.at[j - 1], core, zx_s.at[j - 1])

    def ag_part(a, j):
        pos = (x + 4 - j) % 4
        arrived(g.at[block(pos), acols(a)], agx_r.at[j - 1, a], core, agx_s.at[j - 1, a])
        to_z(pos, a, j)

    def ag_step(a):
        for j in (1, 3, 2):
            ag_part(a, j)

    load_q.wait()
    load_docs.wait()
    for h in range(GROUP):
        part = q[:, h * HEAD : (h + 1) * HEAD]
        q4[h * HEAD : (h + 1) * HEAD, :] = part
        qt[:, h * HEAD : (h + 1) * HEAD] = part.T

    own_pos = lax.broadcasted_iota(jnp.int32, (1, ROWS), 1) + s * ROWS
    start = jnp.zeros((1, ROWS), jnp.int32)
    end = jnp.int32(0)
    for j in range(DOCS):
        end = end + docs_ref[j]
        start = jnp.where(end <= own_pos, jnp.maximum(start, end), start)
    start = jnp.concatenate([start] * GROUP, axis=1)
    key_row = lax.broadcasted_iota(jnp.int32, (ROWS, COLS), 0)
    query_row = lax.broadcasted_iota(jnp.int32, (ROWS, COLS), 1) % ROWS

    def scores(d):
        st = dot(kv[d * ROWS : (d + 1) * ROWS, 0:HEAD], qt[...]) * SCALE
        seen = key_row >= start - (s - d) * ROWS
        if d == 0:
            seen = seen & (key_row <= query_row)
        st = jnp.where(seen, st, -1e30)
        sc[d * ROWS : (d + 1) * ROWS, :] = st
        top = fold(st, jnp.max)
        mx[...] = top if d == 0 else jnp.maximum(mx[...], top)

    def flip_step():
        arrived(kv.at[slot(9 - 7 * zh), :], kv_r.at[9 - 7 * zh], core, kv_s.at[0])
        pass_on(0).start()

        @pl.when(zh == 0)
        def _():
            pass_on(1).start()

    def key_step(hop):
        if hop == 1:

            @pl.when(zh == 0)
            def _():
                arrived(kv.at[slot(2), :], kv_r.at[2], core, kv_s.at[0])
        else:
            arrived(kv.at[slot(2 * hop), :], kv_r.at[2 * hop], core, kv_s.at[0])
        if hop < 4:
            forward(hop - c).start()
        else:

            @pl.when(c == 1)
            def _():
                forward(3).start()

        scores(2 * hop)

    def odd_step(i):
        arrived(kv.at[slot(2 * i + 1), :], kv_r.at[2 * i + 1], core, kf_s.at[i])
        scores(2 * i + 1)

    def ccols(k):
        return pl.ds(k * CW, CW)

    given = {}

    def give(part, k):
        rows = slice(32 * part, 32 * part + 32)
        zs[rows, ccols(k)] = dot(oz[rows, :], w[:, ccols(k)]).astype(BF16)
        given[part, k] = send(
            zs.at[rows, ccols(k)], rz.at[rows, ccols(k)], a_s.at[part, k], a_r.at[part, k], zq if part else zp
        )

    def own(k):
        tb[:, ccols(k)] = dot(mine, w[:, ccols(k)]).astype(BF16)
        if k in XFIRST:
            for to in range(4):

                @pl.when(x != to)
                def _():
                    x_copy(to, k).start()

    def spread(part, k):
        rows = slice(32 * part, 32 * part + 32)
        zs[rows, ccols(k)] = dot(oz[rows, :], w[:, ccols(k)]).astype(BF16)
        for to in (2 * part, 2 * part + 1):

            @pl.when(x != to)
            def _():
                y_copy(to, k).start()

    def y_copy(to, k):
        return pltpu.make_async_remote_copy(
            src_ref=zs.at[to * PART : (to + 1) * PART, ccols(k)],
            dst_ref=yin.at[x, :, ccols(k)],
            send_sem=y_s.at[to, k],
            recv_sem=y_r.at[x, k],
            device_id=at(s, zl * 4 + to),
            device_id_type=MESH,
        )

    def middle(k):
        total = zs[block(x), ccols(k)].astype(F32)
        for j in (1, 3, 2):
            pos = (x + j) % 4
            arrived(yin.at[pos, :, ccols(k)], y_r.at[pos, k], core, y_s.at[pos, k])
            total = total + yin[pos, :, ccols(k)].astype(F32)
        ym[:, ccols(k)] = total.astype(BF16)
        keep(
            ym.at[:, ccols(k)], zin.at[:, ccols(k)], m_s.at[k], m_r.at[k], at(s + (x // 2) * (2 - 4 * zh), tz)
        )

    def attn_grad(a):
        if a == NA - 1:
            ag_last()
        else:
            for pos in range(4):
                arrived(g.at[zblock(pos), acols(a)], agz_r.at[pos, a], zp, agz_s.at[0, a])
        part = dot(g[:, acols(a)], w[:, acols(a)], ((1,), (1,)))
        acc[...] = part if a == 0 else acc[...] + part

    def near(part, k):
        rows = slice(32 * part, 32 * part + 32)
        arrived(rz.at[rows, ccols(k)], a_r.at[part, k], zp, a_s.at[part, k])
        tb[rows, ccols(k)] = (tb[rows, ccols(k)].astype(F32) + rz[rows, ccols(k)].astype(F32)).astype(BF16)
        for to in (2 * part, 2 * part + 1):

            @pl.when(x != to)
            def _():
                x_copy(to, k).start()

    def x_copy(to, k):
        return pltpu.make_async_remote_copy(
            src_ref=tb.at[to * PART : (to + 1) * PART, ccols(k)],
            dst_ref=xin.at[x, :, ccols(k)],
            send_sem=x_s.at[to, k],
            recv_sem=x_r.at[x, k],
            device_id=at(s, zl * 4 + to),
            device_id_type=MESH,
        )

    def finish(k):
        total = tb[block(x), ccols(k)].astype(F32)
        if k in XFIRST:
            arrived(zin.at[:, ccols(k)], m_r.at[k], core, m_s.at[k])
            total = total + zin[:, ccols(k)].astype(F32)
        for j in (1, 3, 2):
            pos = (x + j) % 4
            arrived(xin.at[pos, :, ccols(k)], x_r.at[pos, k], core, x_s.at[pos, k])
            total = total + xin[pos, :, ccols(k)].astype(F32)
        proj_ref[:, ccols(k)] = total.astype(BF16)

    def prepare():
        arrived(do.at[far, :], zh_r.at[1], zhp, zh_s.at[1])
        for h in range(GROUP):
            cols = slice(h * HEAD, (h + 1) * HEAD)
            part = (do[:, cols].astype(F32).T * inv[:, cols]).astype(BF16)
            dost[:, cols] = part
            dos4[cols, :] = part.T
        return jnp.sum(dost[...].astype(F32) * ot[...], axis=0, keepdims=True)

    def back(d, delta):
        rows = slice(d * ROWS, (d + 1) * ROWS)
        slope = dot(kv[rows, HEAD : 2 * HEAD], dost[...])
        p = pr[rows, :]
        ds = (p.astype(F32) * (slope - delta)).astype(BF16)
        dsb[rows, :] = ds
        return dot(ds, q4[...]) * SCALE, dot(p, dos4[...])

    def back_odd(d, delta):
        i = d // 2
        dk, dv = back(d, delta)
        rows = slice(d * ROWS, (d + 1) * ROWS)
        dkv[rows, 0:HEAD] = dk.astype(BF16)
        dkv[rows, HEAD : 2 * HEAD] = dv.astype(BF16)
        keep(dkv.at[rows, :], ci.at[i], ci_s.at[i], ci_r.at[i], core)

    def add_core(i, d):
        arrived(ci.at[i], ci_r.at[i], core, ci_s.at[i])
        rows = slice(d * ROWS, (d + 1) * ROWS)
        dkv[rows, :] = (dkv[rows, :].astype(F32) + ci[i].astype(F32)).astype(BF16)

    def back_even(d, delta):
        hop = d // 2
        dk, dv = back(d, delta)
        rows = slice(d * ROWS, (d + 1) * ROWS)
        dkv[rows, 0:HEAD] = dk.astype(BF16)
        dkv[rows, HEAD : 2 * HEAD] = dv.astype(BF16)
        if hop == 4:
            pl.when(c == 1)(lambda: add_core(3, d))
        elif hop == 0:
            pl.when(c == 0)(lambda: add_core(0, d))
        else:
            add_core(hop - c, d)
        if hop % 2 == 0 and hop > 0:
            i = hop // 2 - 1
            keep(dkv.at[rows, :], ri.at[i], ri_s.at[i], ri_r.at[i], chip_at(6 - 2 * i))

    def hand_back(i):
        return pltpu.make_async_remote_copy(
            src_ref=dkv.at[slot(6 if i else 2 + 4 * zh), :],
            dst_ref=rj.at[i],
            send_sem=rj_s.at[i],
            recv_sem=rj_r.at[i],
            device_id=chip_at(4 if i else 6),
            device_id_type=MESH,
        )

    def flip_back():
        arrived(rj.at[0], rj_r.at[0], core, rj_s.at[0])

        @pl.when(zh == 0)
        def _():
            arrived(rj.at[1], rj_r.at[1], core, rj_s.at[1])
            st[...] = (rj[0].astype(F32) + rj[1].astype(F32)).astype(BF16)

        @pl.when(zh == 1)
        def _():
            st[...] = (rj[0].astype(F32) + dkv[2 * ROWS : 3 * ROWS, :].astype(F32)).astype(BF16)

        keep(st, fi, fi_s.at[0], fi_r.at[0], zhp)

    for a in (NA - 1, *range(NA - 1)):
        to_z(x, a, 0)
    scores(0)
    flip_step()
    key_step(2)
    z_first()
    key_step(4)
    ag_step(0)
    ag_step(1)
    key_step(1)
    key_step(3)
    odd_step(1)
    odd_step(0)
    odd_step(3)
    odd_step(2)
    peak = jnp.max(mx[...], axis=0, keepdims=True)

    def weigh(d, total):
        p = jnp.exp(sc[slot(d), :] - peak)
        pr[slot(d), :] = p.astype(BF16)
        return total + fold(p, jnp.sum)

    total = lax.fori_loop(0, SLOTS, weigh, jnp.zeros((8, COLS), F32))
    inv = 1.0 / jnp.sum(total, axis=0, keepdims=True)
    ot[...] = dot(kv[0 : SLOTS * ROWS, HEAD : 2 * HEAD], pr[...], ((0,), (0,))) * inv
    for h in range(GROUP):
        o[:, h * HEAD : (h + 1) * HEAD] = ot[:, h * HEAD : (h + 1) * HEAD].T.astype(BF16)

    keep(o.at[orow(64 * (1 - zl) + 32, 32), :], oz.at[32:64, :], zh_s.at[0], zh_r.at[0], zhp)

    for k in range(NC):
        load_w[k].wait()

    mine = o[orow(64 * zl, 64), :]

    oz[0:32, :] = o[orow(64 * (1 - zl), 32), :]
    spread(0, 0)
    ag_step(2)
    give(0, 1)
    own(0)
    own(1)
    own(2)
    own(3)
    arrived(oz.at[32:64, :], zh_r.at[0], zhp, zh_s.at[0])
    spread(1, 0)
    give(1, 1)
    attn_grad(0)
    attn_grad(1)
    attn_grad(2)
    attn_grad(3)
    dz[...] = acc[96:128, :].astype(BF16)
    keep(dz, do.at[far, :], zh_s.at[1], zh_r.at[1], zhp)
    do[orow(64 * zl, 64), :] = acc[0:64, :].astype(BF16)
    do[orow(64 * (1 - zl), 32), :] = acc[64:96, :].astype(BF16)
    give(0, 2)
    give(1, 2)
    give(0, 3)
    give(1, 3)
    middle(0)
    near(0, 1)
    near(1, 1)
    delta = prepare()
    back_odd(7, delta)
    back_odd(5, delta)
    back_odd(3, delta)
    back_odd(1, delta)
    back_even(6, delta)
    back_even(2, delta)
    hand_back(0).start()

    @pl.when(zh == 0)
    def _():
        hand_back(1).start()

    near(0, 2)
    back_even(8, delta)
    near(1, 2)
    back_even(4, delta)
    back_even(0, delta)
    near(0, 3)
    flip_back()
    near(1, 3)
    dqt = dot(kv[0 : SLOTS * ROWS, 0:HEAD], dsb[...], ((0,), (0,))) * SCALE
    for h in range(GROUP):
        cols = slice(h * HEAD, (h + 1) * HEAD)
        dq_ref[:, cols] = dqt[:, cols].T.astype(BF16)
    for copy in given.values():
        copy.wait_send()
    for copy in sent:
        copy.wait_send()
    for i in range(4):
        forward(i).wait_send()
    flip().wait_send()
    pass_on(0).wait_send()
    hand_back(0).wait_send()

    @pl.when(zh == 0)
    def _():
        pass_on(1).wait_send()
        hand_back(1).wait_send()

    for to in range(4):

        @pl.when(x != to)
        def _():
            for k in range(NC):
                x_copy(to, k).wait_send()
            for k in XFIRST:
                y_copy(to, k).wait_send()
    for k in range(NC):
        finish(k)

    grad = dkv[0:ROWS, :].astype(F32)
    arrived(fi, fi_r.at[0], zhp, fi_s.at[0])
    grad = grad + fi[...].astype(F32)
    for i in range(2):
        arrived(ri.at[i], ri_r.at[i], core, ri_s.at[i])
        grad = grad + ri[i].astype(F32)
    dk_ref[...] = grad[:, 0:HEAD].astype(BF16)
    dv_ref[...] = grad[:, HEAD : 2 * HEAD].astype(BF16)

def store(*refs):
    copies = [pltpu.make_async_copy(refs[i], refs[4 + i], refs[8].at[i]) for i in range(4)]
    for copy in copies:
        copy.start()
    for copy in copies:
        copy.wait()


def body(queries, key_rows, values, out_weight, out_grad, doc_lengths):
    hbm = pl.BlockSpec(memory_space=pltpu.HBM)
    vmem = pl.BlockSpec(memory_space=pltpu.VMEM)
    dma = pltpu.SemaphoreType.DMA
    scratch = [
        pltpu.SMEM((DOCS,), jnp.int32),
        pltpu.VMEM((COLS, D), BF16),
        pltpu.VMEM((ROWS, D), BF16),
        pltpu.VMEM((ROWS, COLS), BF16),
        pltpu.VMEM((HEAD, COLS), BF16),
        pltpu.VMEM((COLS, HEAD), BF16),
        pltpu.VMEM(((SLOTS + 1) * ROWS, 2 * HEAD), BF16),
        pltpu.VMEM((SLOTS * ROWS, COLS), F32),
        pltpu.VMEM((SLOTS * ROWS, COLS), BF16),
        pltpu.VMEM((8, COLS), F32),
        pltpu.VMEM((HEAD, COLS), F32),
        pltpu.VMEM((ROWS, COLS), BF16),
        pltpu.VMEM((64, COLS), BF16),
        pltpu.VMEM((64, D), BF16),
        pltpu.VMEM((64, D), BF16),
        pltpu.VMEM((64, D), BF16),
        pltpu.VMEM((4, PART, D), BF16),
        pltpu.VMEM((4, PART, D), BF16),
        pltpu.VMEM((PART, D), BF16),
        pltpu.VMEM((PART, D), BF16),
        pltpu.VMEM((ROWS, COLS), F32),
        pltpu.VMEM((ROWS, COLS), BF16),
        pltpu.VMEM((32, COLS), BF16),
        pltpu.VMEM((HEAD, COLS), BF16),
        pltpu.VMEM((COLS, HEAD), BF16),
        pltpu.VMEM((SLOTS * ROWS, COLS), BF16),
        pltpu.VMEM((SLOTS * ROWS, 2 * HEAD), BF16),
        pltpu.VMEM((4, ROWS, 2 * HEAD), BF16),
        pltpu.VMEM((ROWS, 2 * HEAD), BF16),
        pltpu.VMEM((2, ROWS, 2 * HEAD), BF16),
        pltpu.VMEM((2, ROWS, 2 * HEAD), BF16),
        pltpu.VMEM((ROWS, 2 * HEAD), BF16),
        dma((5,)), dma((NC,)),
        dma((3, NA)), dma((3, NA)), dma((4, NA)), dma((4, NA)), dma((3,)), dma((3,)),
        dma((5,)), dma((SLOTS + 1,)), dma((4,)),
        dma((2,)), dma((2,)),
        dma((2, NC)), dma((2, NC)), dma((4, NC)), dma((4, NC)),
        dma((4, NC)), dma((4, NC)), dma((NC,)), dma((NC,)),
        dma((4,)), dma((4,)), dma((1,)), dma((1,)), dma((2,)), dma((2,)), dma((2,)), dma((2,)),
    ]
    shapes = (
        jax.ShapeDtypeStruct((PART, D), BF16),
        jax.ShapeDtypeStruct((ROWS, COLS), BF16),
        jax.ShapeDtypeStruct((ROWS, HEAD), BF16),
        jax.ShapeDtypeStruct((ROWS, HEAD), BF16),
    )
    results = pl.pallas_call(
        kernel,
        out_shape=shapes,
        in_specs=[hbm] * 6,
        out_specs=(vmem,) * 4,
        scratch_shapes=scratch,
        compiler_params=pltpu.CompilerParams(
            collective_id=0, has_side_effects=True, vmem_limit_bytes=63 * 1024 * 1024
        ),
    )(doc_lengths, queries, key_rows, values, out_weight, out_grad)
    return pl.pallas_call(
        store,
        out_shape=shapes,
        in_specs=[vmem] * 4,
        out_specs=(hbm,) * 4,
        scratch_shapes=[dma((4,))],
    )(*results)


def solution(mesh):
    return jax.shard_map(
        body,
        mesh=mesh,
        in_specs=(
            P("seq", "tensor"),
            P("seq", "tensor"),
            P("seq", "tensor"),
            P("tensor", None),
            P(("seq", "tensor"), None),
            P(),
        ),
        out_specs=(
            P(("seq", "tensor"), None),
            P("seq", "tensor"),
            P("seq", "tensor"),
            P("seq", "tensor"),
        ),
        check_vma=False,
    )
```

```python
import math

import jax
import jax.numpy as jnp
from jax import lax
from jax.experimental import pallas as pl
from jax.experimental.pallas import tpu as pltpu
from jax.sharding import PartitionSpec as P

HEAD = 128
GROUP = 4
ROWS = 128
COLS = GROUP * HEAD
D = 8192
DOCS = 12
PART = 16
SLOTS = 9
NA = 4
AW = D // NA
NC = 4
XFIRST = (0,)
CW = D // NC
SCALE = 1.0 / math.sqrt(HEAD)
MESH = pl.DeviceIdType.MESH
F32 = jnp.float32
BF16 = jnp.bfloat16


def dot(a, b, dims=((1,), (0,))):
    return lax.dot_general(a, b, (dims, ((), ())), preferred_element_type=F32)


def fold(a, op):
    return op(a.reshape(a.shape[0] // 8, 8, a.shape[1]), axis=0)


def kernel(
    docs_hbm, q_hbm, k_hbm, v_hbm, w_hbm, g_hbm,
    proj_ref, dq_ref, dk_ref, dv_ref,
    docs_ref, w, g, q, qt, q4, kv, sc, pr, mx, ot, o, oz, zs, rz, tb, xin, yin, ym, zin,
    acc, do, dz, dost, dos4, dsb, dkv, ci, fi, ri, rj, st,
    lsem, wsem,
    agx_s, agx_r, agz_s, agz_r, zx_s, zx_r,
    kv_s, kv_r, kf_s,
    zh_s, zh_r,
    a_s, a_r, x_s, x_r, y_s, y_r, m_s, m_r,
    ci_s, ci_r, fi_s, fi_r, ri_s, ri_r, rj_s, rj_r,
):
    s, t = lax.axis_index("seq"), lax.axis_index("tensor")
    c, chip = s % 2, s // 2
    zh = chip % 2
    zl, x = t // 4, t % 4
    sz = s + 2 - 4 * zh
    tz = t + 4 - 8 * zl

    def at(seq, tensor):
        return {"seq": seq, "tensor": tensor}

    beside = [at(s, zl * 4 + (x + j) % 4) for j in range(4)]
    zp, zq, zhp = at(s, tz), at(sz, tz), at(sz, t)
    core = at(s + 1 - 2 * c, t)

    def chip_at(offset):
        return at(((chip + offset) % 8) * 2 + c, t)

    sent = []

    def send(src, dst, ss, rs, dev):
        copy = pltpu.make_async_remote_copy(
            src_ref=src, dst_ref=dst, send_sem=ss, recv_sem=rs, device_id=dev, device_id_type=MESH
        )
        copy.start()
        return copy

    def keep(*args):
        sent.append(send(*args))

    def arrived(dst, rs, dev, ss):
        pltpu.make_async_remote_copy(
            src_ref=dst, dst_ref=dst, send_sem=ss, recv_sem=rs, device_id=dev, device_id_type=MESH
        ).wait_recv()

    def block(pos):
        return pl.ds(pl.multiple_of(pos * PART, PART), PART)

    left, right, opp = (x + 3) % 4, (x + 1) % 4, (x + 2) % 4

    barrier = pltpu.get_barrier_semaphore()
    friends = beside[1:] + [zp, zq, zhp, core] + [chip_at(j) for j in (2, 4, 6)]
    for dev in friends:
        pl.semaphore_signal(barrier, inc=1, device_id=dev, device_id_type=MESH)

    load_k = pltpu.make_async_copy(k_hbm, kv.at[0:ROWS, 0:HEAD], lsem.at[0])
    load_v = pltpu.make_async_copy(v_hbm, kv.at[0:ROWS, HEAD : 2 * HEAD], lsem.at[1])
    load_g = pltpu.make_async_copy(g_hbm, g.at[block(x), :], lsem.at[2])
    load_q = pltpu.make_async_copy(q_hbm, q, lsem.at[3])
    load_docs = pltpu.make_async_copy(docs_hbm, docs_ref, lsem.at[4])
    load_w = [
        pltpu.make_async_copy(w_hbm.at[:, k * CW : (k + 1) * CW], w.at[:, k * CW : (k + 1) * CW], wsem.at[k])
        for k in range(NC)
    ]
    for copy in [load_k, load_v, load_g, load_q, load_docs] + load_w:
        copy.start()

    load_k.wait()
    load_v.wait()
    load_g.wait()
    pl.semaphore_wait(barrier, len(friends))

    def slot(d):
        return pl.ds(pl.multiple_of(d * ROWS, ROWS), ROWS)

    def forward(i):
        return pltpu.make_async_remote_copy(
            src_ref=kv.at[slot(2 * (i + c)), :],
            dst_ref=kv.at[slot(2 * i + 1), :],
            send_sem=kf_s.at[i],
            recv_sem=kv_r.at[2 * i + 1],
            device_id=core,
            device_id_type=MESH,
        )

    def flip():
        return pltpu.make_async_remote_copy(
            src_ref=kv.at[0:ROWS, :],
            dst_ref=kv.at[slot(2 + 7 * zh), :],
            send_sem=kv_s.at[2],
            recv_sem=kv_r.at[2 + 7 * zh],
            device_id=zhp,
            device_id_type=MESH,
        )

    def pass_on(i):
        return pltpu.make_async_remote_copy(
            src_ref=kv.at[slot(9 - 7 * zh), :],
            dst_ref=kv.at[slot(6 if i else 2 + 4 * zh), :],
            send_sem=kv_s.at[3 + i],
            recv_sem=kv_r.at[6 if i else 2 + 4 * zh],
            device_id=chip_at(4 if i else 2),
            device_id_type=MESH,
        )

    flip().start()
    for i in range(2):
        keep(kv.at[0:ROWS, :], kv.at[slot(4 * i + 4), :], kv_s.at[i], kv_r.at[4 * i + 4], chip_at(2 * i + 2))

    @pl.when(c == 0)
    def _():
        forward(0).start()

    def orow(base, n):
        return pl.ds(pl.multiple_of(base, 32), n)

    far = orow(64 * (1 - zl) + 32, 32)

    def acols(a):
        return pl.ds(a * AW, AW)

    def to_z(pos, a, n):
        keep(
            g.at[block(pos), acols(a)],
            g.at[pl.ds(pl.multiple_of(64 + pos * PART, PART), PART), acols(a)],
            agz_s.at[n, a],
            agz_r.at[pos, a],
            at(s + (pos // 2) * (2 - 4 * zh), tz),
        )

    for a in range(NA):
        for j in range(1, 4):
            keep(g.at[block(x), acols(a)], g.at[block(x), acols(a)], agx_s.at[j - 1, a], agx_r.at[j - 1, a], beside[j])

    def zblock(pos):
        return pl.ds(pl.multiple_of(64 + pos * PART, PART), PART)

    def z_first():
        last = NA - 1
        here = g.at[zblock(x), acols(last)]
        arrived(here, agz_r.at[x, last], zp, agz_s.at[0, last])
        for j in (1, 3, 2):
            keep(here, here, zx_s.at[j - 1], zx_r.at[j - 1], beside[j])

    def ag_last():
        last = NA - 1
        for j in (1, 3, 2):
            pos = (x + 4 - j) % 4
            arrived(g.at[block(pos), acols(last)], agx_r.at[j - 1, last], core, agx_s.at[j - 1, last])
            arrived(g.at[zblock(pos), acols(last)], zx_r.at[j - 1], core, zx_s.at[j - 1])

    def ag_part(a, j):
        pos = (x + 4 - j) % 4
        arrived(g.at[block(pos), acols(a)], agx_r.at[j - 1, a], core, agx_s.at[j - 1, a])
        to_z(pos, a, j)

    def ag_step(a):
        for j in (1, 3, 2):
            ag_part(a, j)

    load_q.wait()
    load_docs.wait()
    for h in range(GROUP):
        part = q[:, h * HEAD : (h + 1) * HEAD]
        q4[h * HEAD : (h + 1) * HEAD, :] = part
        qt[:, h * HEAD : (h + 1) * HEAD] = part.T

    own_pos = lax.broadcasted_iota(jnp.int32, (1, ROWS), 1) + s * ROWS
    start = jnp.zeros((1, ROWS), jnp.int32)
    end = jnp.int32(0)
    for j in range(DOCS):
        end = end + docs_ref[j]
        start = jnp.where(end <= own_pos, jnp.maximum(start, end), start)
    start = jnp.concatenate([start] * GROUP, axis=1)
    key_row = lax.broadcasted_iota(jnp.int32, (ROWS, COLS), 0)
    query_row = lax.broadcasted_iota(jnp.int32, (ROWS, COLS), 1) % ROWS

    def scores(d):
        st = dot(kv[d * ROWS : (d + 1) * ROWS, 0:HEAD], qt[...]) * SCALE
        seen = key_row >= start - (s - d) * ROWS
        if d == 0:
            seen = seen & (key_row <= query_row)
        st = jnp.where(seen, st, -1e30)
        sc[d * ROWS : (d + 1) * ROWS, :] = st
        top = fold(st, jnp.max)
        mx[...] = top if d == 0 else jnp.maximum(mx[...], top)

    def flip_step():
        arrived(kv.at[slot(9 - 7 * zh), :], kv_r.at[9 - 7 * zh], core, kv_s.at[0])
        pass_on(0).start()

        @pl.when(zh == 0)
        def _():
            pass_on(1).start()

    def key_step(hop):
        if hop == 1:

            @pl.when(zh == 0)
            def _():
                arrived(kv.at[slot(2), :], kv_r.at[2], core, kv_s.at[0])
        else:
            arrived(kv.at[slot(2 * hop), :], kv_r.at[2 * hop], core, kv_s.at[0])
        if hop < 4:
            forward(hop - c).start()
        else:

            @pl.when(c == 1)
            def _():
                forward(3).start()

        scores(2 * hop)

    def odd_step(i):
        arrived(kv.at[slot(2 * i + 1), :], kv_r.at[2 * i + 1], core, kf_s.at[i])
        scores(2 * i + 1)

    def ccols(k):
        return pl.ds(k * CW, CW)

    given = {}

    def give(part, k):
        rows = slice(32 * part, 32 * part + 32)
        zs[rows, ccols(k)] = dot(oz[rows, :], w[:, ccols(k)]).astype(BF16)
        given[part, k] = send(
            zs.at[rows, ccols(k)], rz.at[rows, ccols(k)], a_s.at[part, k], a_r.at[part, k], zq if part else zp
        )

    def own(k):
        tb[:, ccols(k)] = dot(mine, w[:, ccols(k)]).astype(BF16)
        if k in XFIRST:
            for to in range(4):

                @pl.when(x != to)
                def _():
                    x_copy(to, k).start()

    def spread(part, k):
        rows = slice(32 * part, 32 * part + 32)
        zs[rows, ccols(k)] = dot(oz[rows, :], w[:, ccols(k)]).astype(BF16)
        for to in (2 * part, 2 * part + 1):

            @pl.when(x != to)
            def _():
                y_copy(to, k).start()

    def y_copy(to, k):
        return pltpu.make_async_remote_copy(
            src_ref=zs.at[to * PART : (to + 1) * PART, ccols(k)],
            dst_ref=yin.at[x, :, ccols(k)],
            send_sem=y_s.at[to, k],
            recv_sem=y_r.at[x, k],
            device_id=at(s, zl * 4 + to),
            device_id_type=MESH,
        )

    def middle(k):
        total = zs[block(x), ccols(k)].astype(F32)
        for j in (1, 3, 2):
            pos = (x + j) % 4
            arrived(yin.at[pos, :, ccols(k)], y_r.at[pos, k], core, y_s.at[pos, k])
            total = total + yin[pos, :, ccols(k)].astype(F32)
        ym[:, ccols(k)] = total.astype(BF16)
        keep(
            ym.at[:, ccols(k)], zin.at[:, ccols(k)], m_s.at[k], m_r.at[k], at(s + (x // 2) * (2 - 4 * zh), tz)
        )

    def attn_grad(a):
        if a == NA - 1:
            ag_last()
        else:
            for pos in range(4):
                arrived(g.at[zblock(pos), acols(a)], agz_r.at[pos, a], zp, agz_s.at[0, a])
        part = dot(g[:, acols(a)], w[:, acols(a)], ((1,), (1,)))
        acc[...] = part if a == 0 else acc[...] + part

    def near(part, k):
        rows = slice(32 * part, 32 * part + 32)
        arrived(rz.at[rows, ccols(k)], a_r.at[part, k], zp, a_s.at[part, k])
        tb[rows, ccols(k)] = (tb[rows, ccols(k)].astype(F32) + rz[rows, ccols(k)].astype(F32)).astype(BF16)
        for to in (2 * part, 2 * part + 1):

            @pl.when(x != to)
            def _():
                x_copy(to, k).start()

    def x_copy(to, k):
        return pltpu.make_async_remote_copy(
            src_ref=tb.at[to * PART : (to + 1) * PART, ccols(k)],
            dst_ref=xin.at[x, :, ccols(k)],
            send_sem=x_s.at[to, k],
            recv_sem=x_r.at[x, k],
            device_id=at(s, zl * 4 + to),
            device_id_type=MESH,
        )

    def finish(k):
        total = tb[block(x), ccols(k)].astype(F32)
        if k in XFIRST:
            arrived(zin.at[:, ccols(k)], m_r.at[k], core, m_s.at[k])
            total = total + zin[:, ccols(k)].astype(F32)
        for j in (1, 3, 2):
            pos = (x + j) % 4
            arrived(xin.at[pos, :, ccols(k)], x_r.at[pos, k], core, x_s.at[pos, k])
            total = total + xin[pos, :, ccols(k)].astype(F32)
        proj_ref[:, ccols(k)] = total.astype(BF16)

    def prepare():
        arrived(do.at[far, :], zh_r.at[1], zhp, zh_s.at[1])
        for h in range(GROUP):
            cols = slice(h * HEAD, (h + 1) * HEAD)
            part = (do[:, cols].astype(F32).T * inv[:, cols]).astype(BF16)
            dost[:, cols] = part
            dos4[cols, :] = part.T
        return jnp.sum(dost[...].astype(F32) * ot[...], axis=0, keepdims=True)

    def back(d, delta):
        rows = slice(d * ROWS, (d + 1) * ROWS)
        slope = dot(kv[rows, HEAD : 2 * HEAD], dost[...])
        p = pr[rows, :]
        ds = (p.astype(F32) * (slope - delta)).astype(BF16)
        dsb[rows, :] = ds
        return dot(ds, q4[...]) * SCALE, dot(p, dos4[...])

    def back_odd(d, delta):
        i = d // 2
        dk, dv = back(d, delta)
        rows = slice(d * ROWS, (d + 1) * ROWS)
        dkv[rows, 0:HEAD] = dk.astype(BF16)
        dkv[rows, HEAD : 2 * HEAD] = dv.astype(BF16)
        keep(dkv.at[rows, :], ci.at[i], ci_s.at[i], ci_r.at[i], core)

    def add_core(i, d):
        arrived(ci.at[i], ci_r.at[i], core, ci_s.at[i])
        rows = slice(d * ROWS, (d + 1) * ROWS)
        dkv[rows, :] = (dkv[rows, :].astype(F32) + ci[i].astype(F32)).astype(BF16)

    def back_even(d, delta):
        hop = d // 2
        dk, dv = back(d, delta)
        rows = slice(d * ROWS, (d + 1) * ROWS)
        dkv[rows, 0:HEAD] = dk.astype(BF16)
        dkv[rows, HEAD : 2 * HEAD] = dv.astype(BF16)
        if hop == 4:
            pl.when(c == 1)(lambda: add_core(3, d))
        elif hop == 0:
            pl.when(c == 0)(lambda: add_core(0, d))
        else:
            add_core(hop - c, d)
        if hop % 2 == 0 and hop > 0:
            i = hop // 2 - 1
            keep(dkv.at[rows, :], ri.at[i], ri_s.at[i], ri_r.at[i], chip_at(6 - 2 * i))

    def hand_back(i):
        return pltpu.make_async_remote_copy(
            src_ref=dkv.at[slot(6 if i else 2 + 4 * zh), :],
            dst_ref=rj.at[i],
            send_sem=rj_s.at[i],
            recv_sem=rj_r.at[i],
            device_id=chip_at(4 if i else 6),
            device_id_type=MESH,
        )

    def flip_back():
        arrived(rj.at[0], rj_r.at[0], core, rj_s.at[0])

        @pl.when(zh == 0)
        def _():
            arrived(rj.at[1], rj_r.at[1], core, rj_s.at[1])
            st[...] = (rj[0].astype(F32) + rj[1].astype(F32)).astype(BF16)

        @pl.when(zh == 1)
        def _():
            st[...] = (rj[0].astype(F32) + dkv[2 * ROWS : 3 * ROWS, :].astype(F32)).astype(BF16)

        keep(st, fi, fi_s.at[0], fi_r.at[0], zhp)

    for a in (NA - 1, *range(NA - 1)):
        to_z(x, a, 0)
    scores(0)
    flip_step()
    key_step(2)
    z_first()
    key_step(4)
    ag_step(0)
    ag_step(1)
    key_step(1)
    key_step(3)
    odd_step(1)
    odd_step(0)
    odd_step(3)
    odd_step(2)
    peak = jnp.max(mx[...], axis=0, keepdims=True)

    def weigh(d, total):
        p = jnp.exp(sc[slot(d), :] - peak)
        pr[slot(d), :] = p.astype(BF16)
        return total + fold(p, jnp.sum)

    total = lax.fori_loop(0, SLOTS, weigh, jnp.zeros((8, COLS), F32))
    inv = 1.0 / jnp.sum(total, axis=0, keepdims=True)
    ot[...] = dot(kv[0 : SLOTS * ROWS, HEAD : 2 * HEAD], pr[...], ((0,), (0,))) * inv
    for h in range(GROUP):
        o[:, h * HEAD : (h + 1) * HEAD] = ot[:, h * HEAD : (h + 1) * HEAD].T.astype(BF16)

    keep(o.at[orow(64 * (1 - zl) + 32, 32), :], oz.at[32:64, :], zh_s.at[0], zh_r.at[0], zhp)

    for k in range(NC):
        load_w[k].wait()

    mine = o[orow(64 * zl, 64), :]

    oz[0:32, :] = o[orow(64 * (1 - zl), 32), :]
    spread(0, 0)
    ag_step(2)
    give(0, 1)
    own(0)
    arrived(oz.at[32:64, :], zh_r.at[0], zhp, zh_s.at[0])
    spread(1, 0)
    give(1, 1)
    own(1)
    own(2)
    own(3)
    attn_grad(0)
    attn_grad(1)
    attn_grad(2)
    attn_grad(3)
    dz[...] = acc[96:128, :].astype(BF16)
    keep(dz, do.at[far, :], zh_s.at[1], zh_r.at[1], zhp)
    do[orow(64 * zl, 64), :] = acc[0:64, :].astype(BF16)
    do[orow(64 * (1 - zl), 32), :] = acc[64:96, :].astype(BF16)
    give(0, 2)
    give(1, 2)
    give(0, 3)
    give(1, 3)
    middle(0)
    near(0, 1)
    near(1, 1)
    delta = prepare()
    back_odd(7, delta)
    back_odd(5, delta)
    back_odd(3, delta)
    back_odd(1, delta)
    back_even(6, delta)
    back_even(2, delta)
    hand_back(0).start()

    @pl.when(zh == 0)
    def _():
        hand_back(1).start()

    near(0, 2)
    back_even(8, delta)
    near(1, 2)
    back_even(4, delta)
    back_even(0, delta)
    near(0, 3)
    flip_back()
    near(1, 3)
    dqt = dot(kv[0 : SLOTS * ROWS, 0:HEAD], dsb[...], ((0,), (0,))) * SCALE
    for h in range(GROUP):
        cols = slice(h * HEAD, (h + 1) * HEAD)
        dq_ref[:, cols] = dqt[:, cols].T.astype(BF16)
    for copy in given.values():
        copy.wait_send()
    for copy in sent:
        copy.wait_send()
    for i in range(4):
        forward(i).wait_send()
    flip().wait_send()
    pass_on(0).wait_send()
    hand_back(0).wait_send()

    @pl.when(zh == 0)
    def _():
        pass_on(1).wait_send()
        hand_back(1).wait_send()

    for to in range(4):

        @pl.when(x != to)
        def _():
            for k in range(NC):
                x_copy(to, k).wait_send()
            for k in XFIRST:
                y_copy(to, k).wait_send()
    for k in range(NC):
        finish(k)

    grad = dkv[0:ROWS, :].astype(F32)
    arrived(fi, fi_r.at[0], zhp, fi_s.at[0])
    grad = grad + fi[...].astype(F32)
    for i in range(2):
        arrived(ri.at[i], ri_r.at[i], core, ri_s.at[i])
        grad = grad + ri[i].astype(F32)
    dk_ref[...] = grad[:, 0:HEAD].astype(BF16)
    dv_ref[...] = grad[:, HEAD : 2 * HEAD].astype(BF16)

def store(*refs):
    copies = [pltpu.make_async_copy(refs[i], refs[4 + i], refs[8].at[i]) for i in range(4)]
    for copy in copies:
        copy.start()
    for copy in copies:
        copy.wait()


def body(queries, key_rows, values, out_weight, out_grad, doc_lengths):
    hbm = pl.BlockSpec(memory_space=pltpu.HBM)
    vmem = pl.BlockSpec(memory_space=pltpu.VMEM)
    dma = pltpu.SemaphoreType.DMA
    scratch = [
        pltpu.SMEM((DOCS,), jnp.int32),
        pltpu.VMEM((COLS, D), BF16),
        pltpu.VMEM((ROWS, D), BF16),
        pltpu.VMEM((ROWS, COLS), BF16),
        pltpu.VMEM((HEAD, COLS), BF16),
        pltpu.VMEM((COLS, HEAD), BF16),
        pltpu.VMEM(((SLOTS + 1) * ROWS, 2 * HEAD), BF16),
        pltpu.VMEM((SLOTS * ROWS, COLS), F32),
        pltpu.VMEM((SLOTS * ROWS, COLS), BF16),
        pltpu.VMEM((8, COLS), F32),
        pltpu.VMEM((HEAD, COLS), F32),
        pltpu.VMEM((ROWS, COLS), BF16),
        pltpu.VMEM((64, COLS), BF16),
        pltpu.VMEM((64, D), BF16),
        pltpu.VMEM((64, D), BF16),
        pltpu.VMEM((64, D), BF16),
        pltpu.VMEM((4, PART, D), BF16),
        pltpu.VMEM((4, PART, D), BF16),
        pltpu.VMEM((PART, D), BF16),
        pltpu.VMEM((PART, D), BF16),
        pltpu.VMEM((ROWS, COLS), F32),
        pltpu.VMEM((ROWS, COLS), BF16),
        pltpu.VMEM((32, COLS), BF16),
        pltpu.VMEM((HEAD, COLS), BF16),
        pltpu.VMEM((COLS, HEAD), BF16),
        pltpu.VMEM((SLOTS * ROWS, COLS), BF16),
        pltpu.VMEM((SLOTS * ROWS, 2 * HEAD), BF16),
        pltpu.VMEM((4, ROWS, 2 * HEAD), BF16),
        pltpu.VMEM((ROWS, 2 * HEAD), BF16),
        pltpu.VMEM((2, ROWS, 2 * HEAD), BF16),
        pltpu.VMEM((2, ROWS, 2 * HEAD), BF16),
        pltpu.VMEM((ROWS, 2 * HEAD), BF16),
        dma((5,)), dma((NC,)),
        dma((3, NA)), dma((3, NA)), dma((4, NA)), dma((4, NA)), dma((3,)), dma((3,)),
        dma((5,)), dma((SLOTS + 1,)), dma((4,)),
        dma((2,)), dma((2,)),
        dma((2, NC)), dma((2, NC)), dma((4, NC)), dma((4, NC)),
        dma((4, NC)), dma((4, NC)), dma((NC,)), dma((NC,)),
        dma((4,)), dma((4,)), dma((1,)), dma((1,)), dma((2,)), dma((2,)), dma((2,)), dma((2,)),
    ]
    shapes = (
        jax.ShapeDtypeStruct((PART, D), BF16),
        jax.ShapeDtypeStruct((ROWS, COLS), BF16),
        jax.ShapeDtypeStruct((ROWS, HEAD), BF16),
        jax.ShapeDtypeStruct((ROWS, HEAD), BF16),
    )
    results = pl.pallas_call(
        kernel,
        out_shape=shapes,
        in_specs=[hbm] * 6,
        out_specs=(vmem,) * 4,
        scratch_shapes=scratch,
        compiler_params=pltpu.CompilerParams(
            collective_id=0, has_side_effects=True, vmem_limit_bytes=63 * 1024 * 1024
        ),
    )(doc_lengths, queries, key_rows, values, out_weight, out_grad)
    return pl.pallas_call(
        store,
        out_shape=shapes,
        in_specs=[vmem] * 4,
        out_specs=(hbm,) * 4,
        scratch_shapes=[dma((4,))],
    )(*results)


def solution(mesh):
    return jax.shard_map(
        body,
        mesh=mesh,
        in_specs=(
            P("seq", "tensor"),
            P("seq", "tensor"),
            P("seq", "tensor"),
            P("tensor", None),
            P(("seq", "tensor"), None),
            P(),
        ),
        out_specs=(
            P(("seq", "tensor"), None),
            P("seq", "tensor"),
            P("seq", "tensor"),
            P("seq", "tensor"),
        ),
        check_vma=False,
    )
```
